32 devices in a mesh: grp: 2 (over y), seq: 4 (over z), row: 2 (over x), col: 2 (over core).
Axes of the slice: x: 2, y: 2, z: 4, core: 2. Of those that a mesh axis runs over, the one named last changes fastest.
Arguments:
- acts: bfloat16 [1024, 4096], P(('grp', 'seq'), ('row', 'col')), parts along dimension 0, may hold values from -6 to 6
- grads: bfloat16 [1024, 4096], P(('grp', 'seq'), ('row', 'col')), parts along dimension 0, may hold values from -0.25 to 0.25
- source_ids: int32 [1024], P(('grp', 'seq')), parts along dimension 0, may hold values from 0 to 7
- basis_in: bfloat16 [4096, 4096], P('seq', ('row', 'col')), may hold values from -0.09375 to 0.09375
- basis_out: bfloat16 [4096, 4096], P('seq', ('row', 'col')), may hold values from -0.09375 to 0.09375
- eigvals: float32 [4096, 4096], P('seq', ('row', 'col')), may hold values from 0.5 to 8
Outputs:
- precond: float32 [8192, 4096], P(('grp', 'seq'), ('row', 'col')), parts along dimension 0
- scores: float32 [1024], P(('grp', 'seq')), parts along dimension 0
- influence: float32 [16], P('grp'), parts along dimension 0
The draws below stay inside these ranges and needn't reach their ends.
There are 2 independent parts, one for each index of `grp`. The reference program is written for one: setup_inputs(seed, part) draws one part's arguments, and reference() takes and returns one part's arrays. A program takes and returns all parts, laid end to end along the dimension named above; an argument that names none is the same for every part. Nothing has to cross between parts.
All inputs are finite; a program needn't handle non-finite values.
Results may differ from the reference program's by a relative error of at most 0.0085.
Values may be sent and summed in bfloat16 or wider, within the bound.
No kernel may reach another device: no remote copies, remote signals or barrier semaphores. Data moves between devices by JAX's collectives and lax.ppermute only.
A program may use at most 128 MiB of HBM per device.

```python
import math
import jax
import jax.numpy as jnp
from jax import lax

D = 4096
TOK_SEQ = 128
SOURCES = 8
TOKENS = 512
N_SEQ = 4


def with_ends(drawn, rng, least, largest):
    longest = drawn.shape.index(max(drawn.shape))
    spots = []
    for shift in (0, 1):
        where = [jax.random.randint(jax.random.fold_in(rng, axis), (), 0, length) for axis, length in enumerate(drawn.shape)]
        where[longest] = (where[longest] + shift) % drawn.shape[longest]
        spots.append(tuple(where))
    return drawn.at[spots[0]].set(least).at[spots[1]].set(largest)


def levels(key, shape, shards, smallest, top_value):
    loudness = 1.0
    for position, parts in shards:
        draws = jax.random.uniform(jax.random.fold_in(jax.random.fold_in(key, 6), position), (parts,), jnp.float32, smallest / len(shards), top_value / len(shards))
        loudness = loudness * jnp.repeat(jnp.exp(draws), shape[position] // parts).reshape((-1,) + (1,) * (len(shape) - 1 - position))
    return loudness


def scatter_about(rng, extent, spread, limit, pieces=(), kind=jnp.bfloat16):
    entries = jax.random.normal(rng, extent, jnp.float32) * spread
    if len(pieces) > 0:
        entries = levels(rng, extent, pieces, -0.22, 0.18) * entries
    return jnp.clip(entries, min=-limit, max=limit).astype(kind)


def setup_inputs(seed: int = 0, part: int = 0) -> dict:
    seeds = jax.random.split(jax.random.key(seed), 7)
    part_keys = jax.random.split(jax.random.fold_in(seeds[6], part), 7)
    return {
        "acts": scatter_about(part_keys[0], (TOKENS, D), 1.0, 6.0, ((0, 4), (1, 4))),
        "grads": scatter_about(part_keys[1], (TOKENS, D), TOKENS ** -0.5, 0.25, ((0, 4), (1, 4))),
        "source_ids": with_ends(jax.random.randint(part_keys[2], (TOKENS,), 0, SOURCES), jax.random.fold_in(part_keys[2], 1), 0, SOURCES - 1).astype(jnp.int32),
        "basis_in": scatter_about(seeds[3], (D, D), D ** -0.5, 0.09375, ((0, 4), (1, 4))),
        "basis_out": scatter_about(seeds[4], (D, D), D ** -0.5, 0.09375, ((0, 4), (1, 4))),
        "eigvals": jnp.clip(jnp.exp(math.log(8.0) - 2.7725887 * jax.random.uniform(seeds[5], (D, D), jnp.float32) ** levels(seeds[5], (D, D), ((0, 4), (1, 4)), -0.2, 0.2)), 0.5, 8.0),
    }


def reference(acts, grads, source_ids, basis_in, basis_out, eigvals):
    rotated_acts = jnp.dot(acts, basis_in, preferred_element_type=jnp.float32).astype(jnp.bfloat16)
    rotated_grads = jnp.dot(grads, basis_out, preferred_element_type=jnp.float32).astype(jnp.bfloat16)
    act_blocks = rotated_acts.reshape(N_SEQ, TOK_SEQ, D)
    grad_blocks = rotated_grads.reshape(N_SEQ, TOK_SEQ, D)

    def add_block(total, pair):
        block_a, block_g = pair
        partial_value = lax.dot_general(block_a, block_g, (((0,), (0,)), ((), ())), preferred_element_type=jnp.float32)
        return total + partial_value.astype(jnp.bfloat16).astype(jnp.float32), None

    outer, unused = lax.scan(add_block, jnp.zeros((D, D), jnp.float32), (act_blocks, grad_blocks))
    precond = outer / eigvals
    precond_rounded = precond.astype(jnp.bfloat16)
    mapped = jnp.dot(rotated_acts, precond_rounded, preferred_element_type=jnp.float32)
    scale_score = float(TOKENS) / float(D * D)
    scores = jnp.sum(mapped * rotated_grads.astype(jnp.float32), axis=1) * scale_score
    onehot = (source_ids[:, None] == jnp.arange(SOURCES, dtype=jnp.int32)[None, :]).astype(jnp.float32)
    influence = jnp.sum(onehot * scores[:, None], axis=0) * (float(SOURCES) / float(TOKENS))
    return precond, scores, influence
```

```python
import jax
import jax.numpy as jnp
from jax import lax
from jax.sharding import PartitionSpec as P

SOURCES = 8
PLANE = ("seq", "row", "col")


def turn(x, pairs):
    return lax.ppermute(x, PLANE, pairs)


def local(acts, grads, source_ids, basis_in, basis_out, eigvals):
    seqs, rows, cols = (lax.axis_size(name) for name in PLANE)
    s = lax.axis_index("seq")
    tok = acts.shape[0]
    total_tokens = tok * seqs
    width = acts.shape[1] * rows * cols
    u = lax.axis_index("col") * rows + lax.axis_index("row")

    def place(seq, block):
        return (seq * rows + block % rows) * cols + block // rows

    def device(seq, feature):
        return seq * rows * cols + feature

    def along(axis, size, step):
        return [(i, i ^ step) for i in range(size)]

    def plane_gather(x):
        held = [x] + [lax.ppermute(x, "row", along("row", rows, j)) for j in range(1, rows)]
        slots = list(held)
        for j in range(1, cols):
            slots += [lax.ppermute(h, "col", along("col", cols, j)) for h in held]
        return slots

    def turned(x):
        pairs = [(device(b, f), place(f, b)) for b in range(seqs) for f in range(rows * cols)]
        return plane_gather(turn(x, pairs))

    def rotate(slots, basis):
        whole = jnp.stack(slots)
        pieces = []
        for k in range(seqs):
            x = lax.dynamic_index_in_dim(whole, u ^ s ^ k, keepdims=False)
            pieces.append(jnp.dot(x, basis, preferred_element_type=jnp.float32).astype(jnp.bfloat16))
        return pieces

    def total(parts):
        out = parts[0].astype(jnp.float32)
        for part in parts[1:]:
            out = out + part.astype(jnp.float32)
        return out

    grad_slots = turned(grads)
    act_slots = turned(acts)
    ids = [source_ids] + [lax.ppermute(source_ids, "seq", along("seq", seqs, k)) for k in range(1, seqs)]

    grad_pieces = rotate(grad_slots, basis_out)
    got = [grad_pieces[0]] + [
        lax.ppermute(grad_pieces[k], "seq", along("seq", seqs, k)) for k in range(1, seqs)
    ]
    own_grads = total(got).astype(jnp.bfloat16)
    rg = [own_grads] + [lax.ppermute(own_grads, "seq", along("seq", seqs, k)) for k in range(1, seqs)]

    act_pieces = rotate(act_slots, basis_in)
    got = []
    for k in range(seqs):
        pairs = [(device(b, f), place(f, b ^ k)) for b in range(seqs) for f in range(rows * cols)]
        got.append(turn(act_pieces[k], pairs))
    own_acts = total(got).astype(jnp.bfloat16)
    whole = jnp.stack(plane_gather(own_acts))
    ra = [lax.dynamic_index_in_dim(whole, u ^ s ^ k, keepdims=False) for k in range(seqs)]

    outer = jnp.zeros(eigvals.shape, jnp.float32)
    for k in range(seqs):
        partial = lax.dot_general(
            ra[k], rg[k], (((0,), (0,)), ((), ())), preferred_element_type=jnp.float32
        )
        outer = outer + partial.astype(jnp.bfloat16).astype(jnp.float32)
    precond = outer / eigvals
    precond_rounded = precond.astype(jnp.bfloat16)
    all_ra, all_rg = jnp.concatenate(ra), jnp.concatenate(rg)
    mapped = lax.dot_general(
        all_rg, precond_rounded, (((1,), (1,)), ((), ())), preferred_element_type=jnp.float32
    )
    partial_value = jnp.sum(mapped * all_ra.astype(jnp.float32), axis=1)
    near = partial_value
    for axis, size in (("col", cols), ("row", rows)):
        near = total([near] + [lax.ppermute(near, axis, along(axis, size, j)) for j in range(1, size)])
    all_ids = jnp.concatenate(ids)
    onehot = (all_ids[:, None] == jnp.arange(SOURCES, dtype=jnp.int32)[None, :]).astype(jnp.float32)
    near_influence = jnp.sum(onehot * near[:, None], axis=0)
    blocks = near.reshape(seqs, tok)
    far = [jnp.concatenate([blocks[k], near_influence]) for k in range(seqs)]
    summed = total([far[0]] + [lax.ppermute(far[k], "seq", along("seq", seqs, k)) for k in range(1, seqs)])
    scale_score = float(total_tokens) / float(width * width)
    scores = summed[:tok] * scale_score
    influence = summed[tok:] * (scale_score * (float(SOURCES) / float(total_tokens)))
    return (precond, scores, influence)


def solution(mesh):
    in_specs = (
        P(("grp", "seq"), ("row", "col")),
        P(("grp", "seq"), ("row", "col")),
        P(("grp", "seq")),
        P("seq", ("row", "col")),
        P("seq", ("row", "col")),
        P("seq", ("row", "col")),
    )
    out_specs = (P(("grp", "seq"), ("row", "col")), P(("grp", "seq")), P("grp"))
    return jax.shard_map(local, mesh=mesh, in_specs=in_specs, out_specs=out_specs, check_vma=False)
```

```python
import jax
import jax.numpy as jnp
from jax import lax
from jax.experimental import pallas as pl
from jax.experimental.pallas import tpu as pltpu
from jax.sharding import PartitionSpec as P

SOURCES = 8
PLANE = ("seq", "row", "col")


def turn(x, pairs):
    return lax.ppermute(x, PLANE, pairs)


def local_any(acts, grads, source_ids, basis_in, basis_out, eigvals):
    seqs, rows, cols = (lax.axis_size(name) for name in PLANE)
    s = lax.axis_index("seq")
    tok = acts.shape[0]
    total_tokens = tok * seqs
    width = acts.shape[1] * rows * cols
    u = lax.axis_index("col") * rows + lax.axis_index("row")

    def place(seq, block):
        return (seq * rows + block % rows) * cols + block // rows

    def device(seq, feature):
        return seq * rows * cols + feature

    def along(axis, size, step):
        return [(i, i ^ step) for i in range(size)]

    def plane_gather(x):
        held = [x] + [lax.ppermute(x, "row", along("row", rows, j)) for j in range(1, rows)]
        slots = list(held)
        for j in range(1, cols):
            slots += [lax.ppermute(h, "col", along("col", cols, j)) for h in held]
        return slots

    def turned(x):
        pairs = [(device(b, f), place(f, b)) for b in range(seqs) for f in range(rows * cols)]
        return plane_gather(turn(x, pairs))

    def rotate(slots, basis):
        whole = jnp.stack(slots)
        pieces = []
        for k in range(seqs):
            x = lax.dynamic_index_in_dim(whole, u ^ s ^ k, keepdims=False)
            pieces.append(jnp.dot(x, basis, preferred_element_type=jnp.float32).astype(jnp.bfloat16))
        return pieces

    def total(parts):
        out = parts[0].astype(jnp.float32)
        for part in parts[1:]:
            out = out + part.astype(jnp.float32)
        return out

    grad_slots = turned(grads)
    act_slots = turned(acts)
    ids = [source_ids] + [lax.ppermute(source_ids, "seq", along("seq", seqs, k)) for k in range(1, seqs)]

    grad_pieces = rotate(grad_slots, basis_out)
    got = [grad_pieces[0]] + [
        lax.ppermute(grad_pieces[k], "seq", along("seq", seqs, k)) for k in range(1, seqs)
    ]
    own_grads = total(got).astype(jnp.bfloat16)
    rg = [own_grads] + [lax.ppermute(own_grads, "seq", along("seq", seqs, k)) for k in range(1, seqs)]

    act_pieces = rotate(act_slots, basis_in)
    got = []
    for k in range(seqs):
        pairs = [(device(b, f), place(f, b ^ k)) for b in range(seqs) for f in range(rows * cols)]
        got.append(turn(act_pieces[k], pairs))
    own_acts = total(got).astype(jnp.bfloat16)
    whole = jnp.stack(plane_gather(own_acts))
    ra = [lax.dynamic_index_in_dim(whole, u ^ s ^ k, keepdims=False) for k in range(seqs)]

    outer = jnp.zeros(eigvals.shape, jnp.float32)
    for k in range(seqs):
        partial = lax.dot_general(
            ra[k], rg[k], (((0,), (0,)), ((), ())), preferred_element_type=jnp.float32
        )
        outer = outer + partial.astype(jnp.bfloat16).astype(jnp.float32)
    precond = outer / eigvals
    precond_rounded = precond.astype(jnp.bfloat16)
    all_ra, all_rg = jnp.concatenate(ra), jnp.concatenate(rg)
    mapped = lax.dot_general(
        all_rg, precond_rounded, (((1,), (1,)), ((), ())), preferred_element_type=jnp.float32
    )
    partial_value = jnp.sum(mapped * all_ra.astype(jnp.float32), axis=1)
    near = partial_value
    for axis, size in (("col", cols), ("row", rows)):
        near = total([near] + [lax.ppermute(near, axis, along(axis, size, j)) for j in range(1, size)])
    all_ids = jnp.concatenate(ids)
    onehot = (all_ids[:, None] == jnp.arange(SOURCES, dtype=jnp.int32)[None, :]).astype(jnp.float32)
    near_influence = jnp.sum(onehot * near[:, None], axis=0)
    blocks = near.reshape(seqs, tok)
    far = [jnp.concatenate([blocks[k], near_influence]) for k in range(seqs)]
    summed = total([far[0]] + [lax.ppermute(far[k], "seq", along("seq", seqs, k)) for k in range(1, seqs)])
    scale_score = float(total_tokens) / float(width * width)
    scores = summed[:tok] * scale_score
    influence = summed[tok:] * (scale_score * (float(SOURCES) / float(total_tokens)))
    return (precond, scores, influence)


def swap(x, axis, step=1):
    return lax.ppermute(x, axis, [(i, i ^ step) for i in range(lax.axis_size(axis))])


def added(a, b):
    return a.astype(jnp.float32) + b.astype(jnp.float32)


def rotate_kernel(order, x0, x1, x2, x3, basis, send, keep, rows):
    step = pl.program_id(0)
    half = pl.num_programs(0) // 2
    tok = x0.shape[0]

    @pl.when(step == 0)
    def _():
        for j, x in enumerate((x0, x1, x2, x3)):
            rows[pl.ds(j * tok, tok), :] = x[...]

    block = jnp.dot(rows[...], basis[...], preferred_element_type=jnp.float32)

    @pl.when(step < half)
    def _():
        send[...] = block.astype(jnp.bfloat16)

    @pl.when(step >= half)
    def _():
        keep[...] = block


def rotate(slots, basis, order):
    tok, depth = slots[0].shape
    blocks = order.shape[0]
    step = basis.shape[1] // blocks
    half = blocks // 2
    rows = tok * len(slots)
    whole = pl.BlockSpec((tok, depth), lambda i, order: (0, 0))
    return pl.pallas_call(
        rotate_kernel,
        out_shape=(
            jax.ShapeDtypeStruct((rows, half * step), jnp.bfloat16),
            jax.ShapeDtypeStruct((rows, half * step), jnp.float32),
        ),
        grid_spec=pltpu.PrefetchScalarGridSpec(
            num_scalar_prefetch=1,
            grid=(blocks,),
            in_specs=[whole] * 4 + [pl.BlockSpec((depth, step), lambda i, order: (0, order[i]))],
            out_specs=(
                pl.BlockSpec((rows, step), lambda i, order: (0, jnp.minimum(i, half - 1))),
                pl.BlockSpec((rows, step), lambda i, order: (0, jnp.maximum(i - half, 0))),
            ),
            scratch_shapes=[pltpu.VMEM((rows, depth), jnp.bfloat16)],
        ),
        compiler_params=pltpu.CompilerParams(vmem_limit_bytes=24 * 2**20),
        cost_estimate=pl.CostEstimate(
            flops=2 * rows * depth * basis.shape[1], bytes_accessed=2 * depth * basis.shape[1], transcendentals=0
        ),
        name="rotate",
    )(order, *slots, basis)


def outer_kernel(place, a0, a1, a2, a3, g, eig, *refs):
    precond, score = refs[-2:]
    step = pl.program_id(0)
    u = place[0]
    tok = g.shape[0] // 4
    piece = a0.shape[1]
    total = None
    for m, a in enumerate((a0, a1, a2, a3)):
        outer = None
        for j in range(4):
            partial = lax.dot_general(
                a[pl.ds((j ^ m) * tok, tok), :],
                g[pl.ds(j * tok, tok), :],
                (((0,), (0,)), ((), ())),
                preferred_element_type=jnp.float32,
            )
            partial = partial.astype(jnp.bfloat16).astype(jnp.float32)
            outer = partial if outer is None else outer + partial
        where = pl.ds(pl.multiple_of((u ^ m) * piece, piece), piece)
        ratio = outer / eig[where, :]
        precond[where, :] = ratio
        mapped = jnp.dot(a[...], ratio.astype(jnp.bfloat16), preferred_element_type=jnp.float32)
        blocks = [mapped[j * tok : (j + 1) * tok] for j in range(4)]
        mapped = jnp.concatenate([blocks[j ^ m] for j in range(4)])
        total = mapped if total is None else total + mapped
    value = total * g[...].astype(jnp.float32)
    lanes = score.shape[1]
    folded = value[:, :lanes]
    for i in range(1, value.shape[1] // lanes):
        folded = folded + value[:, i * lanes : (i + 1) * lanes]

    @pl.when(step == 0)
    def _():
        score[...] = folded

    @pl.when(step > 0)
    def _():
        score[...] += folded


def outer_half(place, acts, grads, eigvals, done=None):
    tokens, piece = acts[0].shape
    width = eigvals.shape[0]
    cols = 256
    steps = grads.shape[1] // cols
    here = lambda i, place: (0, place[1] * steps + i)
    whole = pl.BlockSpec((tokens, piece), lambda i, place: (0, 0))
    in_specs = [whole] * 4 + [
        pl.BlockSpec((tokens, cols), lambda i, place: (0, i)),
        pl.BlockSpec((width, cols), here),
    ]
    args = [place, *acts, grads, eigvals]
    aliases = {}
    if done is not None:
        in_specs.append(pl.BlockSpec(memory_space=pl.ANY))
        aliases = {len(args): 0}
        args.append(done)
    return pl.pallas_call(
        outer_kernel,
        out_shape=(
            jax.ShapeDtypeStruct(eigvals.shape, jnp.float32),
            jax.ShapeDtypeStruct((tokens, 128), jnp.float32),
        ),
        grid_spec=pltpu.PrefetchScalarGridSpec(
            num_scalar_prefetch=1,
            grid=(steps,),
            in_specs=in_specs,
            out_specs=(
                pl.BlockSpec((width, cols), here),
                pl.BlockSpec((tokens, 128), lambda i, place: (0, 0)),
            ),
        ),
        input_output_aliases=aliases,
        compiler_params=pltpu.CompilerParams(vmem_limit_bytes=24 * 2**20),
        cost_estimate=pl.CostEstimate(
            flops=4 * tokens * width * grads.shape[1], bytes_accessed=8 * width * grads.shape[1], transcendentals=0
        ),
        name="outer_half",
    )(*args)


def local_pairs(acts, grads, source_ids, basis_in, basis_out, eigvals):
    seqs, rows, cols = (lax.axis_size(name) for name in PLANE)
    y = lax.axis_index("grp")
    s = lax.axis_index("seq")
    x = lax.axis_index("row")
    k = lax.axis_index("col")
    c = x * cols + k
    u = k * rows + x
    low = s % 2
    tok = acts.shape[0]
    total_tokens = tok * seqs
    block = acts.shape[1]
    width = block * rows * cols
    half, piece = block // 2, block // 4

    def turned(x, flip):
        pairs = []
        for b in range(seqs):
            for f in range(rows * cols):
                pairs.append((b * rows * cols + f, ((f ^ flip) * rows + b % rows) * cols + b // rows))
        return lax.ppermute(x, PLANE, pairs)

    def plane_gather(x):
        near = swap(x, "row")
        return [x, near, swap(x, "col"), swap(near, "col")]

    grads_here = turned(grads, 0)
    acts_here = turned(swap(acts, "row"), cols)

    own = lax.dynamic_slice_in_dim(basis_in, k * half, half, axis=1)
    other = swap(lax.dynamic_slice_in_dim(basis_in, (1 - k) * half, half, axis=1), "col")
    both = jnp.stack([own, other])
    mine = lax.dynamic_slice_in_dim(both, x * piece, piece, axis=2)
    theirs = lax.dynamic_slice(both, (0, y * half, (1 - x) * piece), (2, half, piece))
    first = swap(theirs, "row")
    second = swap(first, "grp")
    upper = jnp.where(y == 0, first, second)
    lower = jnp.where(y == 0, second, first)
    far = jnp.concatenate([upper, lower], axis=1)
    tiles = jnp.concatenate([mine[0], mine[1], far[0], far[1]], axis=1)

    ids = jnp.stack([source_ids] + [swap(source_ids, "seq", j) for j in range(1, seqs)])
    slot_ids = jnp.stack([lax.dynamic_index_in_dim(ids, u ^ s ^ j, keepdims=False) for j in range(seqs)])
    onehot = (slot_ids.reshape(-1, 1) == jnp.arange(SOURCES, dtype=jnp.int32)[None, :]).astype(jnp.float32)

    order_g = jnp.stack([2 - 2 * low, 3 - 2 * low, 2 * low, 2 * low + 1]).astype(jnp.int32)
    send_g, keep_g = rotate(plane_gather(grads_here), basis_out, order_g)
    pair_g = added(keep_g, swap(send_g, "seq", 1)).astype(jnp.bfloat16)
    near_g = added(pair_g, swap(pair_g, "seq", 2)).astype(jnp.bfloat16)
    far_g = swap(near_g, "seq", 1)

    order_a = (jnp.array([1, 3, 0, 2], jnp.int32) ^ (c ^ s)).astype(jnp.int32)
    send_a, keep_a = rotate(plane_gather(acts_here), tiles, order_a)
    got_a = swap(send_a, "seq", 1)
    cross = swap(added(keep_a[:, piece:], got_a[:, piece:]).astype(jnp.bfloat16), "seq", 2)
    own_a = (added(keep_a[:, :piece], got_a[:, :piece]) + cross.astype(jnp.float32)).astype(jnp.bfloat16)
    quarters = plane_gather(own_a)

    precond, near_value = outer_half(jnp.stack([u, low]).astype(jnp.int32), quarters, near_g, eigvals)
    precond, far_value = outer_half(jnp.stack([u, 1 - low]).astype(jnp.int32), quarters, far_g, eigvals, precond)
    value = jnp.sum(near_value + far_value, axis=1)
    part = jnp.sum(onehot * value[:, None], axis=0)
    slots = value.reshape(seqs, tok)
    blocks = jnp.stack([lax.dynamic_index_in_dim(slots, u ^ j, keepdims=False) for j in range(seqs)])
    message = jnp.concatenate([blocks, jnp.broadcast_to(part[None, :], (seqs, SOURCES))], axis=1)
    message = jnp.broadcast_to(message[:, None, :], (seqs, rows * cols, tok + SOURCES))
    message = message.reshape(seqs * rows * cols, tok + SOURCES)
    summed = jnp.sum(lax.all_to_all(message, PLANE, split_axis=0, concat_axis=0, tiled=True), axis=0)
    scale_score = float(total_tokens) / float(width * width)
    scores = summed[:tok] * scale_score
    influence = summed[tok:] * (scale_score * (float(SOURCES) / float(total_tokens)))
    return (precond, scores, influence)


def solution(mesh):
    in_specs = (
        P(("grp", "seq"), ("row", "col")),
        P(("grp", "seq"), ("row", "col")),
        P(("grp", "seq")),
        P("seq", ("row", "col")),
        P("seq", ("row", "col")),
        P("seq", ("row", "col")),
    )
    out_specs = (P(("grp", "seq"), ("row", "col")), P(("grp", "seq")), P("grp"))
    fits = (mesh.shape["seq"], mesh.shape["row"], mesh.shape["col"]) == (4, 2, 2)
    local = local_pairs if fits else local_any
    return jax.shard_map(local, mesh=mesh, in_specs=in_specs, out_specs=out_specs, check_vma=False)
```

```python
import jax
import jax.numpy as jnp
from jax import lax
from jax.experimental import pallas as pl
from jax.experimental.pallas import tpu as pltpu
from jax.sharding import PartitionSpec as P

SOURCES = 8
PLANE = ("seq", "row", "col")


def turn(x, pairs):
    return lax.ppermute(x, PLANE, pairs)


def local_any(acts, grads, source_ids, basis_in, basis_out, eigvals):
    seqs, rows, cols = (lax.axis_size(name) for name in PLANE)
    s = lax.axis_index("seq")
    tok = acts.shape[0]
    total_tokens = tok * seqs
    width = acts.shape[1] * rows * cols
    u = lax.axis_index("col") * rows + lax.axis_index("row")

    def place(seq, block):
        return (seq * rows + block % rows) * cols + block // rows

    def device(seq, feature):
        return seq * rows * cols + feature

    def along(axis, size, step):
        return [(i, i ^ step) for i in range(size)]

    def plane_gather(x):
        held = [x] + [lax.ppermute(x, "row", along("row", rows, j)) for j in range(1, rows)]
        slots = list(held)
        for j in range(1, cols):
            slots += [lax.ppermute(h, "col", along("col", cols, j)) for h in held]
        return slots

    def turned(x):
        pairs = [(device(b, f), place(f, b)) for b in range(seqs) for f in range(rows * cols)]
        return plane_gather(turn(x, pairs))

    def rotate(slots, basis):
        whole = jnp.stack(slots)
        pieces = []
        for k in range(seqs):
            x = lax.dynamic_index_in_dim(whole, u ^ s ^ k, keepdims=False)
            pieces.append(jnp.dot(x, basis, preferred_element_type=jnp.float32).astype(jnp.bfloat16))
        return pieces

    def total(parts):
        out = parts[0].astype(jnp.float32)
        for part in parts[1:]:
            out = out + part.astype(jnp.float32)
        return out

    grad_slots = turned(grads)
    act_slots = turned(acts)
    ids = [source_ids] + [lax.ppermute(source_ids, "seq", along("seq", seqs, k)) for k in range(1, seqs)]

    grad_pieces = rotate(grad_slots, basis_out)
    got = [grad_pieces[0]] + [
        lax.ppermute(grad_pieces[k], "seq", along("seq", seqs, k)) for k in range(1, seqs)
    ]
    own_grads = total(got).astype(jnp.bfloat16)
    rg = [own_grads] + [lax.ppermute(own_grads, "seq", along("seq", seqs, k)) for k in range(1, seqs)]

    act_pieces = rotate(act_slots, basis_in)
    got = []
    for k in range(seqs):
        pairs = [(device(b, f), place(f, b ^ k)) for b in range(seqs) for f in range(rows * cols)]
        got.append(turn(act_pieces[k], pairs))
    own_acts = total(got).astype(jnp.bfloat16)
    whole = jnp.stack(plane_gather(own_acts))
    ra = [lax.dynamic_index_in_dim(whole, u ^ s ^ k, keepdims=False) for k in range(seqs)]

    outer = jnp.zeros(eigvals.shape, jnp.float32)
    for k in range(seqs):
        partial = lax.dot_general(
            ra[k], rg[k], (((0,), (0,)), ((), ())), preferred_element_type=jnp.float32
        )
        outer = outer + partial.astype(jnp.bfloat16).astype(jnp.float32)
    precond = outer / eigvals
    precond_rounded = precond.astype(jnp.bfloat16)
    all_ra, all_rg = jnp.concatenate(ra), jnp.concatenate(rg)
    mapped = lax.dot_general(
        all_rg, precond_rounded, (((1,), (1,)), ((), ())), preferred_element_type=jnp.float32
    )
    partial_value = jnp.sum(mapped * all_ra.astype(jnp.float32), axis=1)
    near = partial_value
    for axis, size in (("col", cols), ("row", rows)):
        near = total([near] + [lax.ppermute(near, axis, along(axis, size, j)) for j in range(1, size)])
    all_ids = jnp.concatenate(ids)
    onehot = (all_ids[:, None] == jnp.arange(SOURCES, dtype=jnp.int32)[None, :]).astype(jnp.float32)
    near_influence = jnp.sum(onehot * near[:, None], axis=0)
    blocks = near.reshape(seqs, tok)
    far = [jnp.concatenate([blocks[k], near_influence]) for k in range(seqs)]
    summed = total([far[0]] + [lax.ppermute(far[k], "seq", along("seq", seqs, k)) for k in range(1, seqs)])
    scale_score = float(total_tokens) / float(width * width)
    scores = summed[:tok] * scale_score
    influence = summed[tok:] * (scale_score * (float(SOURCES) / float(total_tokens)))
    return (precond, scores, influence)


VMEM = 56 * 2**20


def swap(x, axis, step=1):
    return lax.ppermute(x, axis, [(i, i ^ step) for i in range(lax.axis_size(axis))])


def added(a, b):
    return a.astype(jnp.float32) + b.astype(jnp.float32)


def rotate_kernel(order, x0, x1, x2, x3, basis, send, keep, rows):
    tok = x0.shape[0]
    half, step = 2, basis.shape[1] // 4
    for j, x in enumerate((x0, x1, x2, x3)):
        rows[pl.ds(j * tok, tok), :] = x[...]
    for i in range(2 * half):
        where = pl.ds(pl.multiple_of(order[i] * step, step), step)
        block = jnp.dot(rows[...], basis[:, where], preferred_element_type=jnp.float32)
        if i < half:
            send[:, i * step : (i + 1) * step] = block.astype(jnp.bfloat16)
        else:
            keep[:, (i - half) * step : (i - half + 1) * step] = block


def rotate(slots, basis, order):
    tok, depth = slots[0].shape
    rows, cols = tok * len(slots), basis.shape[1]
    vmem = pl.BlockSpec(memory_space=pltpu.VMEM)
    return pl.pallas_call(
        rotate_kernel,
        out_shape=(
            jax.ShapeDtypeStruct((rows, cols // 2), jnp.bfloat16),
            jax.ShapeDtypeStruct((rows, cols // 2), jnp.float32),
        ),
        in_specs=[pl.BlockSpec(memory_space=pltpu.SMEM)] + [vmem] * 5,
        out_specs=(vmem, vmem),
        scratch_shapes=[pltpu.VMEM((rows, depth), jnp.bfloat16)],
        compiler_params=pltpu.CompilerParams(vmem_limit_bytes=24 * 2**20),
        cost_estimate=pl.CostEstimate(flops=2 * rows * depth * cols, bytes_accessed=2 * depth * cols, transcendentals=0),
        name="rotate",
    )(order, *slots, basis)


FEATURE = (0, 2, 1, 3)


def outer_step(place, flat, turned, g, eig, precond, score):
    piece = flat.shape[1] // 4
    total = None
    for m in range(4):
        outer = jnp.dot(turned[pl.ds(m * piece, piece), :], g[...], preferred_element_type=jnp.float32)
        where = pl.ds(pl.multiple_of((place[0] ^ FEATURE[m]) * piece, piece), piece)
        ratio = outer / eig[where, :]
        precond[where, :] = ratio
        mapped = jnp.dot(
            flat[:, m * piece : (m + 1) * piece], ratio.astype(jnp.bfloat16), preferred_element_type=jnp.float32
        )
        total = mapped if total is None else total + mapped
    value = total * g[...].astype(jnp.float32)
    lanes = score.shape[1]
    folded = value[:, :lanes]
    for i in range(1, value.shape[1] // lanes):
        folded = folded + value[:, i * lanes : (i + 1) * lanes]
    step = pl.program_id(0)

    @pl.when(step == 0)
    def _():
        score[...] = folded

    @pl.when(step > 0)
    def _():
        score[...] += folded


def near_kernel(place, a0, a1, a2, a3, g, eig, precond, score, flat, turned):
    tok = g.shape[0] // 4
    piece = a0.shape[1]

    @pl.when(pl.program_id(0) == 0)
    def _():
        for m, a in enumerate((a0, a1, a2, a3)):
            for j in range(4):
                flat[pl.ds(j * tok, tok), m * piece : (m + 1) * piece] = a[pl.ds((j ^ m) * tok, tok), :]
            turned[pl.ds(m * piece, piece), :] = flat[:, m * piece : (m + 1) * piece].T

    outer_step(place, flat, turned, g, eig, precond, score)


def far_kernel(place, flat, turned, g, eig, done, precond, score):
    outer_step(place, flat, turned, g, eig, precond, score)


def outer_half(place, acts, grads, eigvals, done=None):
    width = eigvals.shape[0]
    tokens, cols = grads.shape[0], 256
    steps = grads.shape[1] // cols
    here = lambda i, place: (0, place[1] * steps + i)
    fixed = lambda a: pl.BlockSpec(a.shape, lambda i, place: (0, 0))
    in_specs = [fixed(a) for a in acts] + [
        pl.BlockSpec((tokens, cols), lambda i, place: (0, i)),
        pl.BlockSpec((width, cols), here),
    ]
    out_shape = [
        jax.ShapeDtypeStruct(eigvals.shape, jnp.float32),
        jax.ShapeDtypeStruct((tokens, 128), jnp.float32),
    ]
    out_specs = [pl.BlockSpec((width, cols), here), fixed(out_shape[1])]
    args = [place, *acts, grads, eigvals]
    aliases = {}
    if done is None:
        out_shape += [
            jax.ShapeDtypeStruct((tokens, width), jnp.bfloat16),
            jax.ShapeDtypeStruct((width, tokens), jnp.bfloat16),
        ]
        out_specs += [fixed(out_shape[2]), fixed(out_shape[3])]
    else:
        in_specs.append(pl.BlockSpec(memory_space=pl.ANY))
        aliases = {len(args): 0}
        args.append(done)
    return pl.pallas_call(
        near_kernel if done is None else far_kernel,
        out_shape=out_shape,
        grid_spec=pltpu.PrefetchScalarGridSpec(
            num_scalar_prefetch=1, grid=(steps,), in_specs=in_specs, out_specs=out_specs
        ),
        input_output_aliases=aliases,
        compiler_params=pltpu.CompilerParams(vmem_limit_bytes=VMEM),
        cost_estimate=pl.CostEstimate(
            flops=4 * tokens * width * grads.shape[1], bytes_accessed=8 * width * grads.shape[1], transcendentals=0
        ),
        name="outer_half",
    )(*args)


def local_pairs(acts, grads, source_ids, basis_in, basis_out, eigvals):
    seqs, rows, cols = (lax.axis_size(name) for name in PLANE)
    y = lax.axis_index("grp")
    s = lax.axis_index("seq")
    x = lax.axis_index("row")
    k = lax.axis_index("col")
    c = x * cols + k
    u = k * rows + x
    low = s % 2
    tok = acts.shape[0]
    total_tokens = tok * seqs
    block = acts.shape[1]
    width = block * rows * cols
    half, piece = block // 2, block // 4

    def turned(x):
        pairs = []
        for b in range(seqs):
            for f in range(rows * cols):
                pairs.append((b * rows * cols + f, (f * rows + b % rows) * cols + b // rows))
        return lax.ppermute(x, PLANE, pairs)

    def plane_gather(x):
        near = swap(x, "row")
        return [x, near, swap(x, "col"), swap(near, "col")]

    other = lax.dynamic_slice(basis_in, (y * half, (1 - x) * half), (half, half))
    first = swap(other, "row")
    second = swap(first, "grp")
    upper = jnp.where(y == 0, first, second)
    lower = jnp.where(y == 0, second, first)
    columns = jnp.stack([lax.dynamic_slice_in_dim(basis_in, x * half, half, axis=1), jnp.concatenate([upper, lower])])
    mine = lax.dynamic_slice_in_dim(columns, k * piece, piece, axis=2)
    near = swap(lax.dynamic_slice_in_dim(columns, (1 - k) * piece, piece, axis=2), "col")
    tiles = jnp.concatenate([mine[0], near[0], mine[1], near[1]], axis=1)

    ids = jnp.stack([source_ids] + [swap(source_ids, "seq", j) for j in range(1, seqs)])
    grads_here = turned(grads)
    grads_near, ids = lax.optimization_barrier((swap(grads_here, "col"), ids))
    acts, grads_near = lax.optimization_barrier((acts, grads_near))
    acts_here = turned(acts)
    grads_far = swap(grads_here, "row")
    grad_slots = [grads_here, grads_far, grads_near, swap(grads_far, "col")]

    slot_ids = jnp.stack([lax.dynamic_index_in_dim(ids, u ^ s ^ j, keepdims=False) for j in range(seqs)])
    onehot = (slot_ids.reshape(-1, 1) == jnp.arange(SOURCES, dtype=jnp.int32)[None, :]).astype(jnp.float32)

    order_g = jnp.stack([2 - 2 * low, 3 - 2 * low, 2 * low, 2 * low + 1]).astype(jnp.int32)
    send_g, keep_g = rotate(grad_slots, basis_out, order_g)
    pair_g = added(keep_g, swap(send_g, "seq", 1)).astype(jnp.bfloat16)
    near_g = added(pair_g, swap(pair_g, "seq", 2)).astype(jnp.bfloat16)
    far_g = swap(near_g, "seq", 1)

    order_a = (jnp.array([1, 3, 0, 2], jnp.int32) ^ (c ^ s)).astype(jnp.int32)
    send_a, keep_a = rotate(plane_gather(acts_here), tiles, order_a)
    got_a = swap(send_a, "seq", 1)
    cross = swap(added(keep_a[:, piece:], got_a[:, piece:]).astype(jnp.bfloat16), "seq", 2)
    own_a = (added(keep_a[:, :piece], got_a[:, :piece]) + cross.astype(jnp.float32)).astype(jnp.bfloat16)
    quarters = plane_gather(own_a)

    precond, near_value, flat, across = outer_half(jnp.stack([c, low]).astype(jnp.int32), quarters, near_g, eigvals)
    precond, far_value = outer_half(
        jnp.stack([c, 1 - low]).astype(jnp.int32), (flat, across), far_g, eigvals, precond
    )
    value = jnp.sum(near_value + far_value, axis=1)
    part = jnp.sum(onehot * value[:, None], axis=0)
    slots = value.reshape(seqs, tok)
    blocks = jnp.stack([lax.dynamic_index_in_dim(slots, u ^ j, keepdims=False) for j in range(seqs)])
    message = jnp.concatenate([blocks, jnp.broadcast_to(part[None, :], (seqs, SOURCES))], axis=1)
    message = jnp.broadcast_to(message[:, None, :], (seqs, rows * cols, tok + SOURCES))
    message = message.reshape(seqs * rows * cols, tok + SOURCES)
    summed = jnp.sum(lax.all_to_all(message, PLANE, split_axis=0, concat_axis=0, tiled=True), axis=0)
    scale_score = float(total_tokens) / float(width * width)
    scores = summed[:tok] * scale_score
    influence = summed[tok:] * (scale_score * (float(SOURCES) / float(total_tokens)))
    return (precond, scores, influence)


def solution(mesh):
    in_specs = (
        P(("grp", "seq"), ("row", "col")),
        P(("grp", "seq"), ("row", "col")),
        P(("grp", "seq")),
        P("seq", ("row", "col")),
        P("seq", ("row", "col")),
        P("seq", ("row", "col")),
    )
    out_specs = (P(("grp", "seq"), ("row", "col")), P(("grp", "seq")), P("grp"))
    fits = (mesh.shape["seq"], mesh.shape["row"], mesh.shape["col"]) == (4, 2, 2)
    local = local_pairs if fits else local_any
    return jax.shard_map(local, mesh=mesh, in_specs=in_specs, out_specs=out_specs, check_vma=False)
```

```python
import functools

import jax
import jax.numpy as jnp
from jax import lax
from jax.experimental import pallas as pl
from jax.experimental.pallas import tpu as pltpu
from jax.sharding import PartitionSpec as P

SOURCES = 8
PLANE = ("seq", "row", "col")


def turn(x, pairs):
    return lax.ppermute(x, PLANE, pairs)


def local_any(acts, grads, source_ids, basis_in, basis_out, eigvals):
    seqs, rows, cols = (lax.axis_size(name) for name in PLANE)
    s = lax.axis_index("seq")
    tok = acts.shape[0]
    total_tokens = tok * seqs
    width = acts.shape[1] * rows * cols
    u = lax.axis_index("col") * rows + lax.axis_index("row")

    def place(seq, block):
        return (seq * rows + block % rows) * cols + block // rows

    def device(seq, feature):
        return seq * rows * cols + feature

    def along(axis, size, step):
        return [(i, i ^ step) for i in range(size)]

    def plane_gather(x):
        held = [x] + [lax.ppermute(x, "row", along("row", rows, j)) for j in range(1, rows)]
        slots = list(held)
        for j in range(1, cols):
            slots += [lax.ppermute(h, "col", along("col", cols, j)) for h in held]
        return slots

    def turned(x):
        pairs = [(device(b, f), place(f, b)) for b in range(seqs) for f in range(rows * cols)]
        return plane_gather(turn(x, pairs))

    def rotate(slots, basis):
        whole = jnp.stack(slots)
        pieces = []
        for k in range(seqs):
            x = lax.dynamic_index_in_dim(whole, u ^ s ^ k, keepdims=False)
            pieces.append(jnp.dot(x, basis, preferred_element_type=jnp.float32).astype(jnp.bfloat16))
        return pieces

    def total(parts):
        out = parts[0].astype(jnp.float32)
        for part in parts[1:]:
            out = out + part.astype(jnp.float32)
        return out

    grad_slots = turned(grads)
    act_slots = turned(acts)
    ids = [source_ids] + [lax.ppermute(source_ids, "seq", along("seq", seqs, k)) for k in range(1, seqs)]

    grad_pieces = rotate(grad_slots, basis_out)
    got = [grad_pieces[0]] + [
        lax.ppermute(grad_pieces[k], "seq", along("seq", seqs, k)) for k in range(1, seqs)
    ]
    own_grads = total(got).astype(jnp.bfloat16)
    rg = [own_grads] + [lax.ppermute(own_grads, "seq", along("seq", seqs, k)) for k in range(1, seqs)]

    act_pieces = rotate(act_slots, basis_in)
    got = []
    for k in range(seqs):
        pairs = [(device(b, f), place(f, b ^ k)) for b in range(seqs) for f in range(rows * cols)]
        got.append(turn(act_pieces[k], pairs))
    own_acts = total(got).astype(jnp.bfloat16)
    whole = jnp.stack(plane_gather(own_acts))
    ra = [lax.dynamic_index_in_dim(whole, u ^ s ^ k, keepdims=False) for k in range(seqs)]

    outer = jnp.zeros(eigvals.shape, jnp.float32)
    for k in range(seqs):
        partial = lax.dot_general(
            ra[k], rg[k], (((0,), (0,)), ((), ())), preferred_element_type=jnp.float32
        )
        outer = outer + partial.astype(jnp.bfloat16).astype(jnp.float32)
    precond = outer / eigvals
    precond_rounded = precond.astype(jnp.bfloat16)
    all_ra, all_rg = jnp.concatenate(ra), jnp.concatenate(rg)
    mapped = lax.dot_general(
        all_rg, precond_rounded, (((1,), (1,)), ((), ())), preferred_element_type=jnp.float32
    )
    partial_value = jnp.sum(mapped * all_ra.astype(jnp.float32), axis=1)
    near = partial_value
    for axis, size in (("col", cols), ("row", rows)):
        near = total([near] + [lax.ppermute(near, axis, along(axis, size, j)) for j in range(1, size)])
    all_ids = jnp.concatenate(ids)
    onehot = (all_ids[:, None] == jnp.arange(SOURCES, dtype=jnp.int32)[None, :]).astype(jnp.float32)
    near_influence = jnp.sum(onehot * near[:, None], axis=0)
    blocks = near.reshape(seqs, tok)
    far = [jnp.concatenate([blocks[k], near_influence]) for k in range(seqs)]
    summed = total([far[0]] + [lax.ppermute(far[k], "seq", along("seq", seqs, k)) for k in range(1, seqs)])
    scale_score = float(total_tokens) / float(width * width)
    scores = summed[:tok] * scale_score
    influence = summed[tok:] * (scale_score * (float(SOURCES) / float(total_tokens)))
    return (precond, scores, influence)


VMEM = 16 * 2**20
ROTATE_VMEM = 10 * 2**20
LANES = 128
STAND = 2 * 10**10
BLOCKS = 4


def swap(x, axis, step=1):
    return lax.ppermute(x, axis, [(i, i ^ step) for i in range(lax.axis_size(axis))])


def stand_kernel(x, out):
    out[...] = x[...]


def stand(token, *values):
    token, *values = lax.optimization_barrier((token, *values))
    vmem = pl.BlockSpec(memory_space=pltpu.VMEM)
    token = pl.pallas_call(
        stand_kernel,
        out_shape=jax.ShapeDtypeStruct(token.shape, token.dtype),
        in_specs=[vmem],
        out_specs=vmem,
        compiler_params=pltpu.CompilerParams(vmem_limit_bytes=2**20),
        cost_estimate=pl.CostEstimate(flops=STAND, bytes_accessed=0, transcendentals=0),
        name="stand",
    )(token)
    return token, *values


def added(a, b):
    return a.astype(jnp.float32) + b.astype(jnp.float32)


def rotate_kernel(x0, x1, x2, x3, basis, *refs, notes, flips):
    note, (*sends, keep, rows) = refs[:notes], refs[notes:]
    tok = x0.shape[0]
    for j, x in enumerate((x0, x1, x2, x3)):
        rows[pl.ds(j * tok, tok), :] = x[...]
    at = 0
    for i, out in enumerate((*sends, keep)):
        cut = out.shape[1]
        block = jnp.dot(rows[...], basis[:, at : at + cut], preferred_element_type=jnp.float32)
        for j in range(4):
            k = j ^ (i in flips)
            out[j * tok : (j + 1) * tok, :] = block[k * tok : (k + 1) * tok, :].astype(out.dtype)
        at += cut
    if note:
        sends[0][rows.shape[0] :, :] = note[0][...]


def rotate(slots, basis, messages, *note, flips=()):
    tok, depth = slots[0].shape
    rows, cols = tok * len(slots), basis.shape[1]
    cut = cols // (messages + 1)
    vmem = pl.BlockSpec(memory_space=pltpu.VMEM)
    return pl.pallas_call(
        functools.partial(rotate_kernel, notes=len(note), flips=flips),
        out_shape=[jax.ShapeDtypeStruct((rows + sum(n.shape[0] for n in note), cut), jnp.bfloat16)] * messages
        + [jax.ShapeDtypeStruct((rows, cut), jnp.float32)],
        in_specs=[vmem] * (5 + len(note)),
        out_specs=[vmem] * (messages + 1),
        scratch_shapes=[pltpu.VMEM((rows, depth), jnp.bfloat16)],
        compiler_params=pltpu.CompilerParams(vmem_limit_bytes=ROTATE_VMEM),
        cost_estimate=pl.CostEstimate(flops=2 * rows * depth * cols, bytes_accessed=2 * depth * cols, transcendentals=0),
        name="rotate",
    )(*slots, basis, *note)


def pair_kernel(keep, got, note, out):
    count = keep.shape[0]
    out[:count, :] = (keep[...] + got[:count, :].astype(jnp.float32)).astype(jnp.bfloat16)
    row = lax.broadcasted_iota(jnp.int32, note.shape, 0)
    theirs = jnp.broadcast_to(got[count : count + 1, :].astype(jnp.float32), note.shape)
    out[count:, :] = jnp.where(row == 1, theirs, note[...].astype(jnp.float32)).astype(jnp.bfloat16)


def sum_kernel(pair, across, out):
    count = out.shape[0]
    out[...] = added(pair[:count, :], across[:count, :]).astype(jnp.bfloat16)


def small_call(kernel, rows, *args):
    vmem = pl.BlockSpec(memory_space=pltpu.VMEM)
    shape = (rows, args[0].shape[1])
    return pl.pallas_call(
        kernel,
        out_shape=jax.ShapeDtypeStruct(shape, jnp.bfloat16),
        in_specs=[vmem] * len(args),
        out_specs=vmem,
        compiler_params=pltpu.CompilerParams(vmem_limit_bytes=ROTATE_VMEM),
        cost_estimate=pl.CostEstimate(flops=rows * shape[1], bytes_accessed=8 * rows * shape[1], transcendentals=0),
    )(*args)


def outer_columns(first, flat, turned, g, eig, precond, score, ratio, outs):
    rows = ratio.shape[0] // outs.shape[0]
    where = pl.ds(pl.multiple_of(first, ratio.shape[1]), ratio.shape[1])
    stores = []
    for i in range(outs.shape[0]):
        block = slice(i * rows, (i + 1) * rows)
        outer = jnp.dot(turned[block, :], g[...], preferred_element_type=jnp.float32)
        ratio[block, :] = outer / eig[block, :]
        stores.append(pltpu.make_async_copy(ratio.at[block, :], precond.at[block, where], outs.at[i]))
        stores[-1].start()
    mapped = jnp.dot(flat[...], ratio[...].astype(jnp.bfloat16), preferred_element_type=jnp.float32)
    part = mapped * g[...].astype(jnp.float32)
    folded = score[...]
    for lane in range(0, part.shape[1], score.shape[1]):
        folded = folded + part[:, lane : lane + score.shape[1]]
    score[...] = folded
    for store in stores:
        store.wait()


def near_kernel(
    place, a0, a1, a2, a3, g, eig, precond, score, flat, turned, later, parts, grads, tile, ratio, outs, loads
):
    half = grads.shape[1]
    copies = [pltpu.make_async_copy(a, parts.at[m], loads.at[m]) for m, a in enumerate((a0, a1, a2, a3))]
    copies.append(pltpu.make_async_copy(g, grads, loads.at[4]))
    for i, kept in ((0, tile), (1, later)):
        where = pl.ds(pl.multiple_of(place[1 + i] * half, half), half)
        copies.append(pltpu.make_async_copy(eig.at[:, where], kept, loads.at[5 + i]))
    for copy in copies:
        copy.start()
    tok = parts.shape[1] // 4
    piece = parts.shape[2]
    for m in range(4):
        copies[m].wait()
        where = pl.ds(pl.multiple_of((place[0] ^ m) * piece, piece), piece)
        rows = jnp.concatenate([parts[m, (j ^ m) * tok : ((j ^ m) + 1) * tok, :] for j in range(4)])
        flat[:, where] = rows
        turned[where, :] = rows.T
    score[...] = jnp.zeros_like(score)
    copies[4].wait()
    copies[5].wait()
    outer_columns(
        place[1] * half, flat, turned, grads, tile, precond, score, ratio, outs
    )
    copies[6].wait()


def far_kernel(place, flat, turned, g, eig, done, before, token, precond, value, score, ratio, outs):
    score[...] = before[...]
    outer_columns(
        place[2] * g.shape[1], flat, turned, g, eig, precond, score, ratio, outs
    )
    tok = score.shape[0] // 4
    for j in range(4):
        value[j : j + 1, :] = jnp.sum(score[j * tok : (j + 1) * tok, :].T, axis=0, keepdims=True)


def outer_near(place, acts, grads, eigvals):
    width = eigvals.shape[0]
    tokens, cols = grads.shape
    vmem, hbm = pl.BlockSpec(memory_space=pltpu.VMEM), pl.BlockSpec(memory_space=pltpu.HBM)
    anywhere = pl.BlockSpec(memory_space=pl.ANY)
    return pl.pallas_call(
        near_kernel,
        out_shape=(
            jax.ShapeDtypeStruct(eigvals.shape, jnp.float32),
            jax.ShapeDtypeStruct((tokens, LANES), jnp.float32),
            jax.ShapeDtypeStruct((tokens, width), jnp.bfloat16),
            jax.ShapeDtypeStruct((width, tokens), jnp.bfloat16),
            jax.ShapeDtypeStruct((width, cols), jnp.float32),
        ),
        in_specs=[pl.BlockSpec(memory_space=pltpu.SMEM)] + [anywhere] * 5 + [hbm],
        out_specs=(hbm, vmem, vmem, vmem, vmem),
        scratch_shapes=[
            pltpu.VMEM((4, tokens, width // 4), jnp.bfloat16),
            pltpu.VMEM((tokens, cols), jnp.bfloat16),
            pltpu.VMEM((width, cols), jnp.float32),
            pltpu.VMEM((width, cols), jnp.float32),
            pltpu.SemaphoreType.DMA((BLOCKS,)),
            pltpu.SemaphoreType.DMA((7,)),
        ],
        compiler_params=pltpu.CompilerParams(vmem_limit_bytes=VMEM),
        cost_estimate=pl.CostEstimate(
            flops=4 * tokens * width * cols, bytes_accessed=12 * width * cols, transcendentals=0
        ),
        name="outer_near",
    )(place, *acts, grads, eigvals)


def outer_far(place, flat, turned, grads, eigvals, done, before, token):
    tokens, cols = grads.shape
    width = done.shape[0]
    vmem, hbm = pl.BlockSpec(memory_space=pltpu.VMEM), pl.BlockSpec(memory_space=pltpu.HBM)
    return pl.pallas_call(
        far_kernel,
        out_shape=(
            jax.ShapeDtypeStruct(done.shape, jnp.float32),
            jax.ShapeDtypeStruct((4, tokens // 4), jnp.float32),
        ),
        in_specs=[pl.BlockSpec(memory_space=pltpu.SMEM), vmem, vmem, vmem, vmem, hbm, vmem, vmem],
        out_specs=(hbm, vmem),
        scratch_shapes=[
            pltpu.VMEM((tokens, LANES), jnp.float32),
            pltpu.VMEM((width, cols), jnp.float32),
            pltpu.SemaphoreType.DMA((BLOCKS,)),
        ],
        input_output_aliases={5: 0},
        compiler_params=pltpu.CompilerParams(vmem_limit_bytes=VMEM),
        cost_estimate=pl.CostEstimate(
            flops=4 * tokens * width * cols, bytes_accessed=4 * width * cols, transcendentals=0
        ),
        name="outer_far",
    )(place, flat, turned, grads, eigvals, done, before, token)


def local_pairs(acts, grads, source_ids, basis_in, basis_out, eigvals):
    seqs, rows, cols = (lax.axis_size(name) for name in PLANE)
    s = lax.axis_index("seq")
    x = lax.axis_index("row")
    k = lax.axis_index("col")
    u = k * rows + x
    low, high = s % 2, s // 2
    tok = acts.shape[0]
    total_tokens = tok * seqs
    block = acts.shape[1]
    width = block * rows * cols
    half, piece = block // 2, block // 4

    def turned(x, flip):
        pairs = []
        for b in range(seqs):
            for f in range(rows * cols):
                pairs.append((b * rows * cols + f, ((f ^ flip) * rows + b % rows) * cols + b // rows))
        return lax.ppermute(x, PLANE, pairs)

    def plane_gather(x):
        near = swap(x, "row")
        return [x, near, swap(x, "col"), swap(near, "col")]

    tie = lambda *values: lax.optimization_barrier(values)
    token = jnp.zeros((8, LANES), jnp.float32)
    acts_there = swap(acts, "row")
    grads_here = turned(grads, 0)
    theirs = swap(lax.dynamic_slice_in_dim(basis_in, (1 - k) * half, half, axis=1), "col")
    basis_out = jnp.concatenate(
        [lax.dynamic_slice_in_dim(basis_out, at * half, half, axis=1) for at in (1 - low, low)], axis=1
    )
    note = lambda *ids: jnp.concatenate([jnp.pad(jnp.stack(ids), ((0, 16 - len(ids)), (0, half - tok)))])
    source_ids = source_ids.astype(jnp.bfloat16)
    (token,) = stand(token)
    token, acts_there = tie(token, acts_there)
    acts_here = turned(acts_there, cols)
    (token,) = stand(token)
    token, grads_here, basis_in, basis_out = tie(token, grads_here, basis_in, basis_out)
    grads_far = swap(grads_here, "row")
    mine = lax.dynamic_slice_in_dim(basis_in, k * half, half, axis=1)
    first, second = jnp.where(k == low, mine, theirs), jnp.where(k == low, theirs, mine)
    first, second = (jnp.roll(t, -(1 - x) * piece, axis=1) for t in (first, second))
    tiles = jnp.concatenate([first[:, :piece], second[:, piece:], second[:, :piece], first[:, piece:]], axis=1)
    (token,) = stand(token)
    token, grads_far, tiles, grads_here = tie(token, grads_far, tiles, grads_here)
    grads_both = swap(grads_far, "col")
    grads_near = swap(grads_here, "col")
    token, acts_here = tie(token, acts_here)
    send_g, keep_g = rotate([grads_here, grads_far, grads_near, grads_both], basis_out, 1, note(source_ids))
    got_g = swap(send_g, "seq", 1)
    acts_here, keep_g = tie(acts_here, keep_g)
    acts_far = swap(acts_here, "row")
    token, keep_g = stand(token, keep_g)
    token, acts_far, acts_here = tie(token, acts_far, acts_here)
    acts_both = swap(acts_far, "col")
    acts_near = swap(acts_here, "col")
    to_x, to_pair, to_both, keep_a = rotate([acts_here, acts_far, acts_near, acts_both], tiles, 3, flips=(0, 2))
    from_both = lax.ppermute(
        to_both,
        ("seq", "row"),
        [(i * rows + j, (i ^ 1) * rows + (j ^ 1)) for i in range(seqs) for j in range(rows)],
    )
    from_pair = swap(to_pair, "seq", 1)
    from_x = swap(to_x, "row")
    token, keep_a = tie(token, keep_a)
    token, got_g = tie(token, got_g)
    count = seqs * tok
    pair_g = small_call(pair_kernel, count + 16, keep_g, got_g, note(source_ids))
    token, pair_g = tie(token, pair_g)
    across_g = swap(pair_g, "seq", 2)
    (token,) = stand(token)
    token, from_x, from_pair, from_both = tie(token, from_x, from_pair, from_both)
    same, swapped = added(keep_a, from_pair), added(from_x, from_both)
    stay = jnp.where(x == high, same, swapped)
    cross = swap(jnp.where(x == high, swapped, same).astype(jnp.bfloat16), "seq", 2)
    token, across_g = tie(token, across_g)
    near_g = small_call(sum_kernel, count, pair_g, across_g)
    token, near_g = tie(token, near_g)
    far_g = swap(near_g, "seq", 1)
    (token,) = stand(token)
    token, cross = tie(token, cross)
    own_a = (stay + cross.astype(jnp.float32)).astype(jnp.bfloat16)
    quarters = plane_gather(own_a)

    ids = jnp.stack([source_ids, got_g[count, :tok], across_g[count, :tok], across_g[count + 1, :tok]])
    slot_ids = jnp.stack([lax.dynamic_index_in_dim(ids, u ^ s ^ j, keepdims=False) for j in range(seqs)])
    place = jnp.stack([u, low, 1 - low]).astype(jnp.int32)
    precond, value, flat, across, later = outer_near(place, quarters, near_g, eigvals)
    precond, slots = outer_far(place, flat, across, far_g, later, precond, value, token)
    chosen = slot_ids[None] == jnp.arange(SOURCES, dtype=jnp.bfloat16)[:, None, None]
    part = jnp.sum(jnp.where(chosen, slots[None], 0.0), axis=(1, 2))
    blocks = jnp.stack([lax.dynamic_index_in_dim(slots, u ^ j, keepdims=False) for j in range(seqs)])
    message = jnp.concatenate([blocks, jnp.broadcast_to(part[None, :], (seqs, SOURCES))], axis=1)
    message = jnp.broadcast_to(message[:, None, :], (seqs, rows * cols, tok + SOURCES))
    message = message.reshape(seqs * rows * cols, tok + SOURCES)
    summed = jnp.sum(lax.all_to_all(message, PLANE, split_axis=0, concat_axis=0, tiled=True), axis=0)
    scale_score = float(total_tokens) / float(width * width)
    scores = summed[:tok] * scale_score
    influence = summed[tok:] * (scale_score * (float(SOURCES) / float(total_tokens)))
    return (precond, scores, influence)


def solution(mesh):
    in_specs = (
        P(("grp", "seq"), ("row", "col")),
        P(("grp", "seq"), ("row", "col")),
        P(("grp", "seq")),
        P("seq", ("row", "col")),
        P("seq", ("row", "col")),
        P("seq", ("row", "col")),
    )
    out_specs = (P(("grp", "seq"), ("row", "col")), P(("grp", "seq")), P("grp"))
    fits = (mesh.shape["seq"], mesh.shape["row"], mesh.shape["col"]) == (4, 2, 2)
    local = local_pairs if fits else local_any
    return jax.shard_map(local, mesh=mesh, in_specs=in_specs, out_specs=out_specs, check_vma=False)
```

```python
import functools

import jax
import jax.numpy as jnp
from jax import lax
from jax.experimental import pallas as pl
from jax.experimental.pallas import tpu as pltpu
from jax.sharding import PartitionSpec as P

SOURCES = 8
PLANE = ("seq", "row", "col")


def turn(x, pairs):
    return lax.ppermute(x, PLANE, pairs)


def local_any(acts, grads, source_ids, basis_in, basis_out, eigvals):
    seqs, rows, cols = (lax.axis_size(name) for name in PLANE)
    s = lax.axis_index("seq")
    tok = acts.shape[0]
    total_tokens = tok * seqs
    width = acts.shape[1] * rows * cols
    u = lax.axis_index("col") * rows + lax.axis_index("row")

    def place(seq, block):
        return (seq * rows + block % rows) * cols + block // rows

    def device(seq, feature):
        return seq * rows * cols + feature

    def along(axis, size, step):
        return [(i, i ^ step) for i in range(size)]

    def plane_gather(x):
        held = [x] + [lax.ppermute(x, "row", along("row", rows, j)) for j in range(1, rows)]
        slots = list(held)
        for j in range(1, cols):
            slots += [lax.ppermute(h, "col", along("col", cols, j)) for h in held]
        return slots

    def turned(x):
        pairs = [(device(b, f), place(f, b)) for b in range(seqs) for f in range(rows * cols)]
        return plane_gather(turn(x, pairs))

    def rotate(slots, basis):
        whole = jnp.stack(slots)
        pieces = []
        for k in range(seqs):
            x = lax.dynamic_index_in_dim(whole, u ^ s ^ k, keepdims=False)
            pieces.append(jnp.dot(x, basis, preferred_element_type=jnp.float32).astype(jnp.bfloat16))
        return pieces

    def total(parts):
        out = parts[0].astype(jnp.float32)
        for part in parts[1:]:
            out = out + part.astype(jnp.float32)
        return out

    grad_slots = turned(grads)
    act_slots = turned(acts)
    ids = [source_ids] + [lax.ppermute(source_ids, "seq", along("seq", seqs, k)) for k in range(1, seqs)]

    grad_pieces = rotate(grad_slots, basis_out)
    got = [grad_pieces[0]] + [
        lax.ppermute(grad_pieces[k], "seq", along("seq", seqs, k)) for k in range(1, seqs)
    ]
    own_grads = total(got).astype(jnp.bfloat16)
    rg = [own_grads] + [lax.ppermute(own_grads, "seq", along("seq", seqs, k)) for k in range(1, seqs)]

    act_pieces = rotate(act_slots, basis_in)
    got = []
    for k in range(seqs):
        pairs = [(device(b, f), place(f, b ^ k)) for b in range(seqs) for f in range(rows * cols)]
        got.append(turn(act_pieces[k], pairs))
    own_acts = total(got).astype(jnp.bfloat16)
    whole = jnp.stack(plane_gather(own_acts))
    ra = [lax.dynamic_index_in_dim(whole, u ^ s ^ k, keepdims=False) for k in range(seqs)]

    outer = jnp.zeros(eigvals.shape, jnp.float32)
    for k in range(seqs):
        partial = lax.dot_general(
            ra[k], rg[k], (((0,), (0,)), ((), ())), preferred_element_type=jnp.float32
        )
        outer = outer + partial.astype(jnp.bfloat16).astype(jnp.float32)
    precond = outer / eigvals
    precond_rounded = precond.astype(jnp.bfloat16)
    all_ra, all_rg = jnp.concatenate(ra), jnp.concatenate(rg)
    mapped = lax.dot_general(
        all_rg, precond_rounded, (((1,), (1,)), ((), ())), preferred_element_type=jnp.float32
    )
    partial_value = jnp.sum(mapped * all_ra.astype(jnp.float32), axis=1)
    near = partial_value
    for axis, size in (("col", cols), ("row", rows)):
        near = total([near] + [lax.ppermute(near, axis, along(axis, size, j)) for j in range(1, size)])
    all_ids = jnp.concatenate(ids)
    onehot = (all_ids[:, None] == jnp.arange(SOURCES, dtype=jnp.int32)[None, :]).astype(jnp.float32)
    near_influence = jnp.sum(onehot * near[:, None], axis=0)
    blocks = near.reshape(seqs, tok)
    far = [jnp.concatenate([blocks[k], near_influence]) for k in range(seqs)]
    summed = total([far[0]] + [lax.ppermute(far[k], "seq", along("seq", seqs, k)) for k in range(1, seqs)])
    scale_score = float(total_tokens) / float(width * width)
    scores = summed[:tok] * scale_score
    influence = summed[tok:] * (scale_score * (float(SOURCES) / float(total_tokens)))
    return (precond, scores, influence)


VMEM = 16 * 2**20
NEAR_VMEM = 48 * 2**20
ROTATE_VMEM = 10 * 2**20
LANES = 128
STAND = 2 * 10**10
BLOCKS = 4


def swap(x, axis, step=1):
    return lax.ppermute(x, axis, [(i, i ^ step) for i in range(lax.axis_size(axis))])


def stand_kernel(x, out):
    out[...] = x[...]


def stand(token, *values):
    token, *values = lax.optimization_barrier((token, *values))
    vmem = pl.BlockSpec(memory_space=pltpu.VMEM)
    token = pl.pallas_call(
        stand_kernel,
        out_shape=jax.ShapeDtypeStruct(token.shape, token.dtype),
        in_specs=[vmem],
        out_specs=vmem,
        compiler_params=pltpu.CompilerParams(vmem_limit_bytes=2**20),
        cost_estimate=pl.CostEstimate(flops=STAND, bytes_accessed=0, transcendentals=0),
        name="stand",
    )(token)
    return token, *values


def added(a, b):
    return a.astype(jnp.float32) + b.astype(jnp.float32)


def rotate_kernel(x0, x1, x2, x3, basis, *refs, notes, flips):
    note, (*sends, keep, rows) = refs[:notes], refs[notes:]
    tok = x0.shape[0]
    for j, x in enumerate((x0, x1, x2, x3)):
        rows[pl.ds(j * tok, tok), :] = x[...]
    at = 0
    for i, out in enumerate((*sends, keep)):
        cut = out.shape[1]
        block = jnp.dot(rows[...], basis[:, at : at + cut], preferred_element_type=jnp.float32)
        for j in range(4):
            k = j ^ (i in flips)
            out[j * tok : (j + 1) * tok, :] = block[k * tok : (k + 1) * tok, :].astype(out.dtype)
        at += cut
    if note:
        sends[0][rows.shape[0] :, :] = note[0][...]


def rotate(slots, basis, messages, *note, flips=()):
    tok, depth = slots[0].shape
    rows, cols = tok * len(slots), basis.shape[1]
    cut = cols // (messages + 1)
    vmem = pl.BlockSpec(memory_space=pltpu.VMEM)
    return pl.pallas_call(
        functools.partial(rotate_kernel, notes=len(note), flips=flips),
        out_shape=[jax.ShapeDtypeStruct((rows + sum(n.shape[0] for n in note), cut), jnp.bfloat16)] * messages
        + [jax.ShapeDtypeStruct((rows, cut), jnp.float32)],
        in_specs=[vmem] * (5 + len(note)),
        out_specs=[vmem] * (messages + 1),
        scratch_shapes=[pltpu.VMEM((rows, depth), jnp.bfloat16)],
        compiler_params=pltpu.CompilerParams(vmem_limit_bytes=ROTATE_VMEM),
        cost_estimate=pl.CostEstimate(flops=2 * rows * depth * cols, bytes_accessed=2 * depth * cols, transcendentals=0),
        name="rotate",
    )(*slots, basis, *note)


def pair_kernel(keep, got, note, out):
    count = keep.shape[0]
    out[:count, :] = (keep[...] + got[:count, :].astype(jnp.float32)).astype(jnp.bfloat16)
    row = lax.broadcasted_iota(jnp.int32, note.shape, 0)
    theirs = jnp.broadcast_to(got[count : count + 1, :].astype(jnp.float32), note.shape)
    out[count:, :] = jnp.where(row == 1, theirs, note[...].astype(jnp.float32)).astype(jnp.bfloat16)


def sum_kernel(pair, across, out):
    count = out.shape[0]
    out[...] = added(pair[:count, :], across[:count, :]).astype(jnp.bfloat16)


def small_call(kernel, rows, *args):
    vmem = pl.BlockSpec(memory_space=pltpu.VMEM)
    shape = (rows, args[0].shape[1])
    return pl.pallas_call(
        kernel,
        out_shape=jax.ShapeDtypeStruct(shape, jnp.bfloat16),
        in_specs=[vmem] * len(args),
        out_specs=vmem,
        compiler_params=pltpu.CompilerParams(vmem_limit_bytes=ROTATE_VMEM),
        cost_estimate=pl.CostEstimate(flops=rows * shape[1], bytes_accessed=8 * rows * shape[1], transcendentals=0),
    )(*args)


def outer_columns(first, flat, turned, g, eig, precond, score, ratio, outs):
    rows = ratio.shape[0] // outs.shape[0]
    where = pl.ds(pl.multiple_of(first, ratio.shape[1]), ratio.shape[1])
    stores = []
    for i in range(outs.shape[0]):
        block = slice(i * rows, (i + 1) * rows)
        outer = jnp.dot(turned[block, :], g[...], preferred_element_type=jnp.float32)
        ratio[block, :] = outer / eig[block, :]
        stores.append(pltpu.make_async_copy(ratio.at[block, :], precond.at[block, where], outs.at[i]))
        stores[-1].start()
    mapped = jnp.dot(flat[...], ratio[...].astype(jnp.bfloat16), preferred_element_type=jnp.float32)
    part = mapped * g[...].astype(jnp.float32)
    folded = score[...]
    for lane in range(0, part.shape[1], score.shape[1]):
        folded = folded + part[:, lane : lane + score.shape[1]]
    score[...] = folded
    for store in stores:
        store.wait()


def near_kernel(
    place, a0, a1, a2, a3, g, eig, precond, score, flat, turned, later, parts, grads, tile, ratio, outs, loads
):
    half = grads.shape[1]
    copies = [pltpu.make_async_copy(a, parts.at[m], loads.at[m]) for m, a in enumerate((a0, a1, a2, a3))]
    copies.append(pltpu.make_async_copy(g, grads, loads.at[4]))
    for i, kept in ((0, tile), (1, later)):
        where = pl.ds(pl.multiple_of(place[1 + i] * half, half), half)
        copies.append(pltpu.make_async_copy(eig.at[:, where], kept, loads.at[5 + i]))
    for copy in copies:
        copy.start()
    tok = parts.shape[1] // 4
    piece = parts.shape[2]
    for m in range(4):
        copies[m].wait()
        where = pl.ds(pl.multiple_of((place[0] ^ m) * piece, piece), piece)
        rows = jnp.concatenate([parts[m, (j ^ m) * tok : ((j ^ m) + 1) * tok, :] for j in range(4)])
        flat[:, where] = rows
        turned[where, :] = rows.T
    score[...] = jnp.zeros_like(score)
    copies[4].wait()
    copies[5].wait()
    outer_columns(
        place[1] * half, flat, turned, grads, tile, precond, score, ratio, outs
    )
    copies[6].wait()


def far_kernel(place, flat, turned, g, eig, done, before, token, precond, value, score, ratio, outs):
    score[...] = before[...]
    outer_columns(
        place[2] * g.shape[1], flat, turned, g, eig, precond, score, ratio, outs
    )
    tok = score.shape[0] // 4
    for j in range(4):
        value[j : j + 1, :] = jnp.sum(score[j * tok : (j + 1) * tok, :].T, axis=0, keepdims=True)


def outer_near(place, acts, grads, eigvals):
    width = eigvals.shape[0]
    tokens, cols = grads.shape
    vmem, hbm = pl.BlockSpec(memory_space=pltpu.VMEM), pl.BlockSpec(memory_space=pltpu.HBM)
    anywhere = pl.BlockSpec(memory_space=pl.ANY)
    return pl.pallas_call(
        near_kernel,
        out_shape=(
            jax.ShapeDtypeStruct(eigvals.shape, jnp.float32),
            jax.ShapeDtypeStruct((tokens, LANES), jnp.float32),
            jax.ShapeDtypeStruct((tokens, width), jnp.bfloat16),
            jax.ShapeDtypeStruct((width, tokens), jnp.bfloat16),
            jax.ShapeDtypeStruct((width, cols), jnp.float32),
        ),
        in_specs=[pl.BlockSpec(memory_space=pltpu.SMEM)] + [anywhere] * 5 + [hbm],
        out_specs=(hbm, vmem, vmem, vmem, vmem),
        scratch_shapes=[
            pltpu.VMEM((4, tokens, width // 4), jnp.bfloat16),
            pltpu.VMEM((tokens, cols), jnp.bfloat16),
            pltpu.VMEM((width, cols), jnp.float32),
            pltpu.VMEM((width, cols), jnp.float32),
            pltpu.SemaphoreType.DMA((BLOCKS,)),
            pltpu.SemaphoreType.DMA((7,)),
        ],
        compiler_params=pltpu.CompilerParams(vmem_limit_bytes=NEAR_VMEM),
        cost_estimate=pl.CostEstimate(
            flops=4 * tokens * width * cols, bytes_accessed=12 * width * cols, transcendentals=0
        ),
        name="outer_near",
    )(place, *acts, grads, eigvals)


def outer_far(place, flat, turned, grads, eigvals, done, before, token):
    tokens, cols = grads.shape
    width = done.shape[0]
    vmem, hbm = pl.BlockSpec(memory_space=pltpu.VMEM), pl.BlockSpec(memory_space=pltpu.HBM)
    return pl.pallas_call(
        far_kernel,
        out_shape=(
            jax.ShapeDtypeStruct(done.shape, jnp.float32),
            jax.ShapeDtypeStruct((4, tokens // 4), jnp.float32),
        ),
        in_specs=[pl.BlockSpec(memory_space=pltpu.SMEM), vmem, vmem, vmem, vmem, hbm, vmem, vmem],
        out_specs=(hbm, vmem),
        scratch_shapes=[
            pltpu.VMEM((tokens, LANES), jnp.float32),
            pltpu.VMEM((width, cols), jnp.float32),
            pltpu.SemaphoreType.DMA((BLOCKS,)),
        ],
        input_output_aliases={5: 0},
        compiler_params=pltpu.CompilerParams(vmem_limit_bytes=VMEM),
        cost_estimate=pl.CostEstimate(
            flops=4 * tokens * width * cols, bytes_accessed=4 * width * cols, transcendentals=0
        ),
        name="outer_far",
    )(place, flat, turned, grads, eigvals, done, before, token)


def local_pairs(acts, grads, source_ids, basis_in, basis_out, eigvals):
    seqs, rows, cols = (lax.axis_size(name) for name in PLANE)
    s = lax.axis_index("seq")
    x = lax.axis_index("row")
    k = lax.axis_index("col")
    u = k * rows + x
    low, high = s % 2, s // 2
    tok = acts.shape[0]
    total_tokens = tok * seqs
    block = acts.shape[1]
    width = block * rows * cols
    half, piece = block // 2, block // 4

    def turned(x):
        pairs = []
        for b in range(seqs):
            for f in range(rows * cols):
                pairs.append((b * rows * cols + f, (f * rows + b % rows) * cols + b // rows))
        return lax.ppermute(x, PLANE, pairs)

    def plane_gather(x):
        near = swap(x, "row")
        return [x, near, swap(x, "col"), swap(near, "col")]

    tie = lambda *values: lax.optimization_barrier(values)
    token = jnp.zeros((8, LANES), jnp.float32)
    grads_here = turned(grads)
    theirs = swap(lax.dynamic_slice_in_dim(basis_in, (1 - k) * half, half, axis=1), "col")
    basis_out = jnp.concatenate(
        [lax.dynamic_slice_in_dim(basis_out, at * half, half, axis=1) for at in (1 - low, low)], axis=1
    )
    note = lambda *ids: jnp.concatenate([jnp.pad(jnp.stack(ids), ((0, 16 - len(ids)), (0, half - tok)))])
    source_ids = source_ids.astype(jnp.bfloat16)
    (token,) = stand(token)
    token, grads_here, basis_in, basis_out, acts = tie(token, grads_here, basis_in, basis_out, acts)
    acts_here = turned(acts)
    grads_far = swap(grads_here, "row")
    mine = lax.dynamic_slice_in_dim(basis_in, k * half, half, axis=1)
    first, second = jnp.where(k == low, mine, theirs), jnp.where(k == low, theirs, mine)
    first, second = (jnp.roll(t, -(1 - x) * piece, axis=1) for t in (first, second))
    tiles = jnp.concatenate([first[:, :piece], second[:, piece:], second[:, :piece], first[:, piece:]], axis=1)
    (token,) = stand(token)
    token, grads_far, tiles, grads_here = tie(token, grads_far, tiles, grads_here)
    grads_both = swap(grads_far, "col")
    grads_near = swap(grads_here, "col")
    token, acts_here = tie(token, acts_here)
    send_g, keep_g = rotate([grads_here, grads_far, grads_near, grads_both], basis_out, 1, note(source_ids))
    got_g = swap(send_g, "seq", 1)
    acts_here, keep_g = tie(acts_here, keep_g)
    acts_far = swap(acts_here, "row")
    token, keep_g = stand(token, keep_g)
    token, acts_far, acts_here = tie(token, acts_far, acts_here)
    acts_both = swap(acts_far, "col")
    acts_near = swap(acts_here, "col")
    to_x, to_pair, to_both, keep_a = rotate([acts_here, acts_far, acts_near, acts_both], tiles, 3, flips=(0, 2))
    from_both = lax.ppermute(
        to_both,
        ("seq", "row"),
        [(i * rows + j, (i ^ 1) * rows + (j ^ 1)) for i in range(seqs) for j in range(rows)],
    )
    from_pair = swap(to_pair, "seq", 1)
    from_x = swap(to_x, "row")
    token, keep_a = tie(token, keep_a)
    token, got_g = tie(token, got_g)
    count = seqs * tok
    pair_g = small_call(pair_kernel, count + 16, keep_g, got_g, note(source_ids))
    token, pair_g = tie(token, pair_g)
    across_g = swap(pair_g, "seq", 2)
    (token,) = stand(token)
    token, from_x, from_pair, from_both = tie(token, from_x, from_pair, from_both)
    same, swapped = added(keep_a, from_pair), added(from_x, from_both)
    stay = jnp.where(x == high, same, swapped)
    cross = swap(jnp.where(x == high, swapped, same).astype(jnp.bfloat16), "seq", 2)
    token, across_g = tie(token, across_g)
    near_g = small_call(sum_kernel, count, pair_g, across_g)
    token, near_g = tie(token, near_g)
    far_g = swap(near_g, "seq", 1)
    (token,) = stand(token)
    token, cross = tie(token, cross)
    own_a = (stay + cross.astype(jnp.float32)).astype(jnp.bfloat16)
    quarters = plane_gather(own_a)

    ids = jnp.stack([source_ids, got_g[count, :tok], across_g[count, :tok], across_g[count + 1, :tok]])
    slot_ids = jnp.stack([lax.dynamic_index_in_dim(ids, u ^ s ^ j, keepdims=False) for j in range(seqs)])
    place = jnp.stack([u, low, 1 - low]).astype(jnp.int32)
    precond, value, flat, across, later = outer_near(place, quarters, near_g, eigvals)
    precond, slots = outer_far(place, flat, across, far_g, later, precond, value, token)
    chosen = slot_ids[None] == jnp.arange(SOURCES, dtype=jnp.bfloat16)[:, None, None]
    part = jnp.sum(jnp.where(chosen, slots[None], 0.0), axis=(1, 2))
    blocks = jnp.stack([lax.dynamic_index_in_dim(slots, u ^ j, keepdims=False) for j in range(seqs)])
    message = jnp.concatenate([blocks, jnp.broadcast_to(part[None, :], (seqs, SOURCES))], axis=1)
    message = jnp.broadcast_to(message[:, None, :], (seqs, rows * cols, tok + SOURCES))
    message = message.reshape(seqs * rows * cols, tok + SOURCES)
    summed = jnp.sum(lax.all_to_all(message, PLANE, split_axis=0, concat_axis=0, tiled=True), axis=0)
    scale_score = float(total_tokens) / float(width * width)
    scores = summed[:tok] * scale_score
    influence = summed[tok:] * (scale_score * (float(SOURCES) / float(total_tokens)))
    return (precond, scores, influence)


def solution(mesh):
    in_specs = (
        P(("grp", "seq"), ("row", "col")),
        P(("grp", "seq"), ("row", "col")),
        P(("grp", "seq")),
        P("seq", ("row", "col")),
        P("seq", ("row", "col")),
        P("seq", ("row", "col")),
    )
    out_specs = (P(("grp", "seq"), ("row", "col")), P(("grp", "seq")), P("grp"))
    fits = (mesh.shape["seq"], mesh.shape["row"], mesh.shape["col"]) == (4, 2, 2)
    local = local_pairs if fits else local_any
    return jax.shard_map(local, mesh=mesh, in_specs=in_specs, out_specs=out_specs, check_vma=False)
```

```python
import functools

import jax
import jax.numpy as jnp
from jax import lax
from jax.experimental import pallas as pl
from jax.experimental.pallas import tpu as pltpu
from jax.sharding import PartitionSpec as P

SOURCES = 8
PLANE = ("seq", "row", "col")


def turn(x, pairs):
    return lax.ppermute(x, PLANE, pairs)


def local_any(acts, grads, source_ids, basis_in, basis_out, eigvals):
    seqs, rows, cols = (lax.axis_size(name) for name in PLANE)
    s = lax.axis_index("seq")
    tok = acts.shape[0]
    total_tokens = tok * seqs
    width = acts.shape[1] * rows * cols
    u = lax.axis_index("col") * rows + lax.axis_index("row")

    def place(seq, block):
        return (seq * rows + block % rows) * cols + block // rows

    def device(seq, feature):
        return seq * rows * cols + feature

    def along(axis, size, step):
        return [(i, i ^ step) for i in range(size)]

    def plane_gather(x):
        held = [x] + [lax.ppermute(x, "row", along("row", rows, j)) for j in range(1, rows)]
        slots = list(held)
        for j in range(1, cols):
            slots += [lax.ppermute(h, "col", along("col", cols, j)) for h in held]
        return slots

    def turned(x):
        pairs = [(device(b, f), place(f, b)) for b in range(seqs) for f in range(rows * cols)]
        return plane_gather(turn(x, pairs))

    def rotate(slots, basis):
        whole = jnp.stack(slots)
        pieces = []
        for k in range(seqs):
            x = lax.dynamic_index_in_dim(whole, u ^ s ^ k, keepdims=False)
            pieces.append(jnp.dot(x, basis, preferred_element_type=jnp.float32).astype(jnp.bfloat16))
        return pieces

    def total(parts):
        out = parts[0].astype(jnp.float32)
        for part in parts[1:]:
            out = out + part.astype(jnp.float32)
        return out

    grad_slots = turned(grads)
    act_slots = turned(acts)
    ids = [source_ids] + [lax.ppermute(source_ids, "seq", along("seq", seqs, k)) for k in range(1, seqs)]

    grad_pieces = rotate(grad_slots, basis_out)
    got = [grad_pieces[0]] + [
        lax.ppermute(grad_pieces[k], "seq", along("seq", seqs, k)) for k in range(1, seqs)
    ]
    own_grads = total(got).astype(jnp.bfloat16)
    rg = [own_grads] + [lax.ppermute(own_grads, "seq", along("seq", seqs, k)) for k in range(1, seqs)]

    act_pieces = rotate(act_slots, basis_in)
    got = []
    for k in range(seqs):
        pairs = [(device(b, f), place(f, b ^ k)) for b in range(seqs) for f in range(rows * cols)]
        got.append(turn(act_pieces[k], pairs))
    own_acts = total(got).astype(jnp.bfloat16)
    whole = jnp.stack(plane_gather(own_acts))
    ra = [lax.dynamic_index_in_dim(whole, u ^ s ^ k, keepdims=False) for k in range(seqs)]

    outer = jnp.zeros(eigvals.shape, jnp.float32)
    for k in range(seqs):
        partial = lax.dot_general(
            ra[k], rg[k], (((0,), (0,)), ((), ())), preferred_element_type=jnp.float32
        )
        outer = outer + partial.astype(jnp.bfloat16).astype(jnp.float32)
    precond = outer / eigvals
    precond_rounded = precond.astype(jnp.bfloat16)
    all_ra, all_rg = jnp.concatenate(ra), jnp.concatenate(rg)
    mapped = lax.dot_general(
        all_rg, precond_rounded, (((1,), (1,)), ((), ())), preferred_element_type=jnp.float32
    )
    partial_value = jnp.sum(mapped * all_ra.astype(jnp.float32), axis=1)
    near = partial_value
    for axis, size in (("col", cols), ("row", rows)):
        near = total([near] + [lax.ppermute(near, axis, along(axis, size, j)) for j in range(1, size)])
    all_ids = jnp.concatenate(ids)
    onehot = (all_ids[:, None] == jnp.arange(SOURCES, dtype=jnp.int32)[None, :]).astype(jnp.float32)
    near_influence = jnp.sum(onehot * near[:, None], axis=0)
    blocks = near.reshape(seqs, tok)
    far = [jnp.concatenate([blocks[k], near_influence]) for k in range(seqs)]
    summed = total([far[0]] + [lax.ppermute(far[k], "seq", along("seq", seqs, k)) for k in range(1, seqs)])
    scale_score = float(total_tokens) / float(width * width)
    scores = summed[:tok] * scale_score
    influence = summed[tok:] * (scale_score * (float(SOURCES) / float(total_tokens)))
    return (precond, scores, influence)


VMEM = 16 * 2**20
NEAR_VMEM = 48 * 2**20
ROTATE_VMEM = 10 * 2**20
LANES = 128
STAND = 2 * 10**10
BLOCKS = 4


def swap(x, axis, step=1):
    return lax.ppermute(x, axis, [(i, i ^ step) for i in range(lax.axis_size(axis))])


def stand_kernel(x, out):
    out[...] = x[...]


def stand(token, *values):
    token, *values = lax.optimization_barrier((token, *values))
    vmem = pl.BlockSpec(memory_space=pltpu.VMEM)
    token = pl.pallas_call(
        stand_kernel,
        out_shape=jax.ShapeDtypeStruct(token.shape, token.dtype),
        in_specs=[vmem],
        out_specs=vmem,
        compiler_params=pltpu.CompilerParams(vmem_limit_bytes=2**20),
        cost_estimate=pl.CostEstimate(flops=STAND, bytes_accessed=0, transcendentals=0),
        name="stand",
    )(token)
    return token, *values


def added(a, b):
    return a.astype(jnp.float32) + b.astype(jnp.float32)


def rotate_kernel(x0, x1, x2, x3, basis, *refs, notes, flips):
    note, (*sends, keep, rows) = refs[:notes], refs[notes:]
    tok = x0.shape[0]
    for j, x in enumerate((x0, x1, x2, x3)):
        rows[pl.ds(j * tok, tok), :] = x[...]
    at = 0
    for i, out in enumerate((*sends, keep)):
        cut = out.shape[1]
        block = jnp.dot(rows[...], basis[:, at : at + cut], preferred_element_type=jnp.float32)
        for j in range(4):
            k = j ^ (i in flips)
            out[j * tok : (j + 1) * tok, :] = block[k * tok : (k + 1) * tok, :].astype(out.dtype)
        at += cut
    if note:
        sends[0][rows.shape[0] :, :] = note[0][...]


def rotate(slots, basis, messages, *note, flips=()):
    tok, depth = slots[0].shape
    rows, cols = tok * len(slots), basis.shape[1]
    cut = cols // (messages + 1)
    vmem = pl.BlockSpec(memory_space=pltpu.VMEM)
    return pl.pallas_call(
        functools.partial(rotate_kernel, notes=len(note), flips=flips),
        out_shape=[jax.ShapeDtypeStruct((rows + sum(n.shape[0] for n in note), cut), jnp.bfloat16)] * messages
        + [jax.ShapeDtypeStruct((rows, cut), jnp.float32)],
        in_specs=[vmem] * (5 + len(note)),
        out_specs=[vmem] * (messages + 1),
        scratch_shapes=[pltpu.VMEM((rows, depth), jnp.bfloat16)],
        compiler_params=pltpu.CompilerParams(vmem_limit_bytes=ROTATE_VMEM),
        cost_estimate=pl.CostEstimate(flops=2 * rows * depth * cols, bytes_accessed=2 * depth * cols, transcendentals=0),
        name="rotate",
    )(*slots, basis, *note)


def pair_kernel(keep, got, note, out):
    count = keep.shape[0]
    out[:count, :] = (keep[...] + got[:count, :].astype(jnp.float32)).astype(jnp.bfloat16)
    row = lax.broadcasted_iota(jnp.int32, note.shape, 0)
    theirs = jnp.broadcast_to(got[count : count + 1, :].astype(jnp.float32), note.shape)
    out[count:, :] = jnp.where(row == 1, theirs, note[...].astype(jnp.float32)).astype(jnp.bfloat16)


def sum_kernel(pair, across, out):
    count = out.shape[0]
    out[...] = added(pair[:count, :], across[:count, :]).astype(jnp.bfloat16)


def small_call(kernel, rows, *args):
    vmem = pl.BlockSpec(memory_space=pltpu.VMEM)
    shape = (rows, args[0].shape[1])
    return pl.pallas_call(
        kernel,
        out_shape=jax.ShapeDtypeStruct(shape, jnp.bfloat16),
        in_specs=[vmem] * len(args),
        out_specs=vmem,
        compiler_params=pltpu.CompilerParams(vmem_limit_bytes=ROTATE_VMEM),
        cost_estimate=pl.CostEstimate(flops=rows * shape[1], bytes_accessed=8 * rows * shape[1], transcendentals=0),
    )(*args)


def outer_columns(first, flat, turned, g, eig, precond, score, ratio, outs):
    rows = ratio.shape[0] // outs.shape[0]
    where = pl.ds(pl.multiple_of(first, ratio.shape[1]), ratio.shape[1])
    stores = []
    for i in range(outs.shape[0]):
        block = slice(i * rows, (i + 1) * rows)
        outer = jnp.dot(turned[block, :], g[...], preferred_element_type=jnp.float32)
        ratio[block, :] = outer / eig[block, :]
        stores.append(pltpu.make_async_copy(ratio.at[block, :], precond.at[block, where], outs.at[i]))
        stores[-1].start()
    mapped = jnp.dot(flat[...], ratio[...].astype(jnp.bfloat16), preferred_element_type=jnp.float32)
    part = mapped * g[...].astype(jnp.float32)
    folded = score[...]
    for lane in range(0, part.shape[1], score.shape[1]):
        folded = folded + part[:, lane : lane + score.shape[1]]
    score[...] = folded
    for store in stores:
        store.wait()


def near_kernel(
    place, a0, a1, a2, a3, g, eig, precond, score, flat, turned, later, parts, grads, tile, ratio, outs, loads
):
    half = grads.shape[1]
    copies = [pltpu.make_async_copy(a, parts.at[m], loads.at[m]) for m, a in enumerate((a0, a1, a2, a3))]
    copies.append(pltpu.make_async_copy(g, grads, loads.at[4]))
    for i, kept in ((0, tile), (1, later)):
        where = pl.ds(pl.multiple_of(place[1 + i] * half, half), half)
        copies.append(pltpu.make_async_copy(eig.at[:, where], kept, loads.at[5 + i]))
    for copy in copies:
        copy.start()
    tok = parts.shape[1] // 4
    piece = parts.shape[2]
    for m in range(4):
        copies[m].wait()
        where = pl.ds(pl.multiple_of((place[0] ^ m) * piece, piece), piece)
        rows = jnp.concatenate([parts[m, (j ^ m) * tok : ((j ^ m) + 1) * tok, :] for j in range(4)])
        flat[:, where] = rows
        turned[where, :] = rows.T
    score[...] = jnp.zeros_like(score)
    copies[4].wait()
    copies[5].wait()
    outer_columns(
        place[1] * half, flat, turned, grads, tile, precond, score, ratio, outs
    )
    copies[6].wait()


def far_kernel(place, flat, turned, g, eig, done, before, token, precond, value, score, ratio, outs):
    score[...] = before[...]
    outer_columns(
        place[2] * g.shape[1], flat, turned, g, eig, precond, score, ratio, outs
    )
    tok = score.shape[0] // 4
    for j in range(4):
        value[j : j + 1, :] = jnp.sum(score[j * tok : (j + 1) * tok, :].T, axis=0, keepdims=True)


def finish_kernel(scale_score, scale_influence, parts, scores, influence):
    tok = scores.shape[0]
    scores[...] = jnp.sum(parts[:, :tok], axis=0) * scale_score
    influence[...] = jnp.sum(parts[:, tok:], axis=0) * scale_influence


def outer_near(place, acts, grads, eigvals):
    width = eigvals.shape[0]
    tokens, cols = grads.shape
    vmem, hbm = pl.BlockSpec(memory_space=pltpu.VMEM), pl.BlockSpec(memory_space=pltpu.HBM)
    anywhere = pl.BlockSpec(memory_space=pl.ANY)
    return pl.pallas_call(
        near_kernel,
        out_shape=(
            jax.ShapeDtypeStruct(eigvals.shape, jnp.float32),
            jax.ShapeDtypeStruct((tokens, LANES), jnp.float32),
            jax.ShapeDtypeStruct((tokens, width), jnp.bfloat16),
            jax.ShapeDtypeStruct((width, tokens), jnp.bfloat16),
            jax.ShapeDtypeStruct((width, cols), jnp.float32),
        ),
        in_specs=[pl.BlockSpec(memory_space=pltpu.SMEM)] + [anywhere] * 5 + [hbm],
        out_specs=(hbm, vmem, vmem, vmem, vmem),
        scratch_shapes=[
            pltpu.VMEM((4, tokens, width // 4), jnp.bfloat16),
            pltpu.VMEM((tokens, cols), jnp.bfloat16),
            pltpu.VMEM((width, cols), jnp.float32),
            pltpu.VMEM((width, cols), jnp.float32),
            pltpu.SemaphoreType.DMA((BLOCKS,)),
            pltpu.SemaphoreType.DMA((7,)),
        ],
        compiler_params=pltpu.CompilerParams(vmem_limit_bytes=NEAR_VMEM),
        cost_estimate=pl.CostEstimate(
            flops=4 * tokens * width * cols, bytes_accessed=12 * width * cols, transcendentals=0
        ),
        name="outer_near",
    )(place, *acts, grads, eigvals)


def outer_far(place, flat, turned, grads, eigvals, done, before, token):
    tokens, cols = grads.shape
    width = done.shape[0]
    vmem, hbm = pl.BlockSpec(memory_space=pltpu.VMEM), pl.BlockSpec(memory_space=pltpu.HBM)
    return pl.pallas_call(
        far_kernel,
        out_shape=(
            jax.ShapeDtypeStruct(done.shape, jnp.float32),
            jax.ShapeDtypeStruct((4, tokens // 4), jnp.float32),
        ),
        in_specs=[pl.BlockSpec(memory_space=pltpu.SMEM), vmem, vmem, vmem, vmem, hbm, vmem, vmem],
        out_specs=(hbm, vmem),
        scratch_shapes=[
            pltpu.VMEM((tokens, LANES), jnp.float32),
            pltpu.VMEM((width, cols), jnp.float32),
            pltpu.SemaphoreType.DMA((BLOCKS,)),
        ],
        input_output_aliases={5: 0},
        compiler_params=pltpu.CompilerParams(vmem_limit_bytes=VMEM),
        cost_estimate=pl.CostEstimate(
            flops=4 * tokens * width * cols, bytes_accessed=4 * width * cols, transcendentals=0
        ),
        name="outer_far",
    )(place, flat, turned, grads, eigvals, done, before, token)


def local_pairs(acts, grads, source_ids, basis_in, basis_out, eigvals):
    seqs, rows, cols = (lax.axis_size(name) for name in PLANE)
    s = lax.axis_index("seq")
    x = lax.axis_index("row")
    k = lax.axis_index("col")
    u = k * rows + x
    low, high = s % 2, s // 2
    tok = acts.shape[0]
    total_tokens = tok * seqs
    block = acts.shape[1]
    width = block * rows * cols
    half, piece = block // 2, block // 4

    def turned(x, flip):
        pairs = []
        for b in range(seqs):
            for f in range(rows * cols):
                pairs.append((b * rows * cols + f, ((f ^ flip) * rows + b % rows) * cols + b // rows))
        return lax.ppermute(x, PLANE, pairs)

    def plane_gather(x):
        near = swap(x, "row")
        return [x, near, swap(x, "col"), swap(near, "col")]

    tie = lambda *values: lax.optimization_barrier(values)
    token = jnp.zeros((8, LANES), jnp.float32)
    acts_there = swap(acts, "row")
    grads_here = turned(grads, 0)
    theirs = swap(lax.dynamic_slice_in_dim(basis_in, (1 - k) * half, half, axis=1), "col")
    basis_out = jnp.concatenate(
        [lax.dynamic_slice_in_dim(basis_out, at * half, half, axis=1) for at in (1 - low, low)], axis=1
    )
    note = lambda *ids: jnp.concatenate([jnp.pad(jnp.stack(ids), ((0, 16 - len(ids)), (0, half - tok)))])
    source_ids = source_ids.astype(jnp.bfloat16)
    acts_here = turned(acts_there, cols)
    (token,) = stand(token)
    token, grads_here, basis_in, basis_out = tie(token, grads_here, basis_in, basis_out)
    grads_far = swap(grads_here, "row")
    mine = lax.dynamic_slice_in_dim(basis_in, k * half, half, axis=1)
    first, second = jnp.where(k == low, mine, theirs), jnp.where(k == low, theirs, mine)
    first, second = (jnp.roll(t, -(1 - x) * piece, axis=1) for t in (first, second))
    tiles = jnp.concatenate([second[:, piece:], second[:, :piece], first[:, :piece], first[:, piece:]], axis=1)
    (token,) = stand(token)
    token, grads_far, tiles, grads_here = tie(token, grads_far, tiles, grads_here)
    grads_both = swap(grads_far, "col")
    grads_near = swap(grads_here, "col")
    token, acts_here = tie(token, acts_here)
    send_g, keep_g = rotate([grads_here, grads_far, grads_near, grads_both], basis_out, 1, note(source_ids))
    got_g = swap(send_g, "seq", 1)
    acts_here, keep_g = tie(acts_here, keep_g)
    acts_far = swap(acts_here, "row")
    token, keep_g = stand(token, keep_g)
    token, acts_far, acts_here = tie(token, acts_far, acts_here)
    acts_both = swap(acts_far, "col")
    acts_near = swap(acts_here, "col")
    to_pair, to_both, to_x, keep_a = rotate([acts_here, acts_far, acts_near, acts_both], tiles, 3, flips=(1, 2))
    from_both = lax.ppermute(
        to_both,
        ("seq", "row"),
        [(i * rows + j, (i ^ 1) * rows + (j ^ 1)) for i in range(seqs) for j in range(rows)],
    )
    from_pair = swap(to_pair, "seq", 1)
    from_x = swap(to_x, "row")
    token, keep_a = tie(token, keep_a)
    token, got_g = tie(token, got_g)
    count = seqs * tok
    pair_g = small_call(pair_kernel, count + 16, keep_g, got_g, note(source_ids))
    token, pair_g = tie(token, pair_g)
    across_g = swap(pair_g, "seq", 2)
    (token,) = stand(token)
    token, from_x, from_pair, from_both = tie(token, from_x, from_pair, from_both)
    same, swapped = added(keep_a, from_pair), added(from_x, from_both)
    stay = jnp.where(x == high, same, swapped)
    cross = swap(jnp.where(x == high, swapped, same).astype(jnp.bfloat16), "seq", 2)
    token, across_g = tie(token, across_g)
    near_g = small_call(sum_kernel, count, pair_g, across_g)
    token, near_g = tie(token, near_g)
    far_g = swap(near_g, "seq", 1)
    (token,) = stand(token)
    token, cross = tie(token, cross)
    own_a = (stay + cross.astype(jnp.float32)).astype(jnp.bfloat16)
    quarters = plane_gather(own_a)

    ids = jnp.stack([source_ids, got_g[count, :tok], across_g[count, :tok], across_g[count + 1, :tok]])
    slot_ids = jnp.stack([lax.dynamic_index_in_dim(ids, u ^ s ^ j, keepdims=False) for j in range(seqs)])
    place = jnp.stack([u, low, 1 - low]).astype(jnp.int32)
    precond, value, flat, across, later = outer_near(place, quarters, near_g, eigvals)
    precond, slots = outer_far(place, flat, across, far_g, later, precond, value, token)
    chosen = slot_ids[None] == jnp.arange(SOURCES, dtype=jnp.bfloat16)[:, None, None]
    part = jnp.sum(jnp.where(chosen, slots[None], 0.0), axis=(1, 2))
    blocks = jnp.stack([lax.dynamic_index_in_dim(slots, u ^ j, keepdims=False) for j in range(seqs)])
    message = jnp.concatenate([blocks, jnp.broadcast_to(part[None, :], (seqs, SOURCES))], axis=1)
    message = jnp.broadcast_to(message[:, None, :], (seqs, rows * cols, tok + SOURCES))
    message = message.reshape(seqs * rows * cols, tok + SOURCES)
    parts = lax.all_to_all(message, PLANE, split_axis=0, concat_axis=0, tiled=True)
    scale_score = float(total_tokens) / float(width * width)
    vmem = pl.BlockSpec(memory_space=pltpu.VMEM)
    scores, influence = pl.pallas_call(
        functools.partial(finish_kernel, scale_score, scale_score * (float(SOURCES) / float(total_tokens))),
        out_shape=(jax.ShapeDtypeStruct((tok,), jnp.float32), jax.ShapeDtypeStruct((SOURCES,), jnp.float32)),
        in_specs=[vmem],
        out_specs=(vmem, vmem),
        compiler_params=pltpu.CompilerParams(vmem_limit_bytes=2**20),
        name="finish",
    )(parts)
    return (precond, scores, influence)


def solution(mesh):
    in_specs = (
        P(("grp", "seq"), ("row", "col")),
        P(("grp", "seq"), ("row", "col")),
        P(("grp", "seq")),
        P("seq", ("row", "col")),
        P("seq", ("row", "col")),
        P("seq", ("row", "col")),
    )
    out_specs = (P(("grp", "seq"), ("row", "col")), P(("grp", "seq")), P("grp"))
    fits = (mesh.shape["seq"], mesh.shape["row"], mesh.shape["col"]) == (4, 2, 2)
    local = local_pairs if fits else local_any
    return jax.shard_map(local, mesh=mesh, in_specs=in_specs, out_specs=out_specs, check_vma=False)
```

```python
import functools

import jax
import jax.numpy as jnp
from jax import lax
from jax.experimental import pallas as pl
from jax.experimental.pallas import tpu as pltpu
from jax.sharding import PartitionSpec as P

SOURCES = 8
PLANE = ("seq", "row", "col")


def turn(x, pairs):
    return lax.ppermute(x, PLANE, pairs)


def local_any(acts, grads, source_ids, basis_in, basis_out, eigvals):
    seqs, rows, cols = (lax.axis_size(name) for name in PLANE)
    s = lax.axis_index("seq")
    tok = acts.shape[0]
    total_tokens = tok * seqs
    width = acts.shape[1] * rows * cols
    u = lax.axis_index("col") * rows + lax.axis_index("row")

    def place(seq, block):
        return (seq * rows + block % rows) * cols + block // rows

    def device(seq, feature):
        return seq * rows * cols + feature

    def along(axis, size, step):
        return [(i, i ^ step) for i in range(size)]

    def plane_gather(x):
        held = [x] + [lax.ppermute(x, "row", along("row", rows, j)) for j in range(1, rows)]
        slots = list(held)
        for j in range(1, cols):
            slots += [lax.ppermute(h, "col", along("col", cols, j)) for h in held]
        return slots

    def turned(x):
        pairs = [(device(b, f), place(f, b)) for b in range(seqs) for f in range(rows * cols)]
        return plane_gather(turn(x, pairs))

    def rotate(slots, basis):
        whole = jnp.stack(slots)
        pieces = []
        for k in range(seqs):
            x = lax.dynamic_index_in_dim(whole, u ^ s ^ k, keepdims=False)
            pieces.append(jnp.dot(x, basis, preferred_element_type=jnp.float32).astype(jnp.bfloat16))
        return pieces

    def total(parts):
        out = parts[0].astype(jnp.float32)
        for part in parts[1:]:
            out = out + part.astype(jnp.float32)
        return out

    grad_slots = turned(grads)
    act_slots = turned(acts)
    ids = [source_ids] + [lax.ppermute(source_ids, "seq", along("seq", seqs, k)) for k in range(1, seqs)]

    grad_pieces = rotate(grad_slots, basis_out)
    got = [grad_pieces[0]] + [
        lax.ppermute(grad_pieces[k], "seq", along("seq", seqs, k)) for k in range(1, seqs)
    ]
    own_grads = total(got).astype(jnp.bfloat16)
    rg = [own_grads] + [lax.ppermute(own_grads, "seq", along("seq", seqs, k)) for k in range(1, seqs)]

    act_pieces = rotate(act_slots, basis_in)
    got = []
    for k in range(seqs):
        pairs = [(device(b, f), place(f, b ^ k)) for b in range(seqs) for f in range(rows * cols)]
        got.append(turn(act_pieces[k], pairs))
    own_acts = total(got).astype(jnp.bfloat16)
    whole = jnp.stack(plane_gather(own_acts))
    ra = [lax.dynamic_index_in_dim(whole, u ^ s ^ k, keepdims=False) for k in range(seqs)]

    outer = jnp.zeros(eigvals.shape, jnp.float32)
    for k in range(seqs):
        partial = lax.dot_general(
            ra[k], rg[k], (((0,), (0,)), ((), ())), preferred_element_type=jnp.float32
        )
        outer = outer + partial.astype(jnp.bfloat16).astype(jnp.float32)
    precond = outer / eigvals
    precond_rounded = precond.astype(jnp.bfloat16)
    all_ra, all_rg = jnp.concatenate(ra), jnp.concatenate(rg)
    mapped = lax.dot_general(
        all_rg, precond_rounded, (((1,), (1,)), ((), ())), preferred_element_type=jnp.float32
    )
    partial_value = jnp.sum(mapped * all_ra.astype(jnp.float32), axis=1)
    near = partial_value
    for axis, size in (("col", cols), ("row", rows)):
        near = total([near] + [lax.ppermute(near, axis, along(axis, size, j)) for j in range(1, size)])
    all_ids = jnp.concatenate(ids)
    onehot = (all_ids[:, None] == jnp.arange(SOURCES, dtype=jnp.int32)[None, :]).astype(jnp.float32)
    near_influence = jnp.sum(onehot * near[:, None], axis=0)
    blocks = near.reshape(seqs, tok)
    far = [jnp.concatenate([blocks[k], near_influence]) for k in range(seqs)]
    summed = total([far[0]] + [lax.ppermute(far[k], "seq", along("seq", seqs, k)) for k in range(1, seqs)])
    scale_score = float(total_tokens) / float(width * width)
    scores = summed[:tok] * scale_score
    influence = summed[tok:] * (scale_score * (float(SOURCES) / float(total_tokens)))
    return (precond, scores, influence)


VMEM = 16 * 2**20
NEAR_VMEM = 48 * 2**20
ROTATE_VMEM = 10 * 2**20
LANES = 128
STAND = 2 * 10**10
BLOCKS = 4


def swap(x, axis, step=1):
    return lax.ppermute(x, axis, [(i, i ^ step) for i in range(lax.axis_size(axis))])


def stand_kernel(x, out):
    out[...] = x[...]


def stand(token, *values):
    token, *values = lax.optimization_barrier((token, *values))
    vmem = pl.BlockSpec(memory_space=pltpu.VMEM)
    token = pl.pallas_call(
        stand_kernel,
        out_shape=jax.ShapeDtypeStruct(token.shape, token.dtype),
        in_specs=[vmem],
        out_specs=vmem,
        compiler_params=pltpu.CompilerParams(vmem_limit_bytes=2**20),
        cost_estimate=pl.CostEstimate(flops=STAND, bytes_accessed=0, transcendentals=0),
        name="stand",
    )(token)
    return token, *values


def added(a, b):
    return a.astype(jnp.float32) + b.astype(jnp.float32)


def rotate_kernel(x0, x1, x2, x3, basis, *refs, notes, flips):
    note, (*sends, keep, rows) = refs[:notes], refs[notes:]
    tok = x0.shape[0]
    for j, x in enumerate((x0, x1, x2, x3)):
        rows[pl.ds(j * tok, tok), :] = x[...]
    at = 0
    for i, out in enumerate((*sends, keep)):
        cut = out.shape[1]
        block = jnp.dot(rows[...], basis[:, at : at + cut], preferred_element_type=jnp.float32)
        for j in range(4):
            k = j ^ (i in flips)
            out[j * tok : (j + 1) * tok, :] = block[k * tok : (k + 1) * tok, :].astype(out.dtype)
        at += cut
    if note:
        sends[0][rows.shape[0] :, :] = note[0][...]


def rotate(slots, basis, messages, *note, flips=()):
    tok, depth = slots[0].shape
    rows, cols = tok * len(slots), basis.shape[1]
    cut = cols // (messages + 1)
    vmem = pl.BlockSpec(memory_space=pltpu.VMEM)
    return pl.pallas_call(
        functools.partial(rotate_kernel, notes=len(note), flips=flips),
        out_shape=[jax.ShapeDtypeStruct((rows + sum(n.shape[0] for n in note), cut), jnp.bfloat16)] * messages
        + [jax.ShapeDtypeStruct((rows, cut), jnp.float32)],
        in_specs=[vmem] * (5 + len(note)),
        out_specs=[vmem] * (messages + 1),
        scratch_shapes=[pltpu.VMEM((rows, depth), jnp.bfloat16)],
        compiler_params=pltpu.CompilerParams(vmem_limit_bytes=ROTATE_VMEM),
        cost_estimate=pl.CostEstimate(flops=2 * rows * depth * cols, bytes_accessed=2 * depth * cols, transcendentals=0),
        name="rotate",
    )(*slots, basis, *note)


def pair_kernel(keep, got, note, out):
    count = keep.shape[0]
    out[:count, :] = (keep[...] + got[:count, :].astype(jnp.float32)).astype(jnp.bfloat16)
    row = lax.broadcasted_iota(jnp.int32, note.shape, 0)
    theirs = jnp.broadcast_to(got[count:, :].astype(jnp.float32)[:1], note.shape)
    out[count:, :] = jnp.where(row == 1, theirs, note[...].astype(jnp.float32)).astype(jnp.bfloat16)


def sum_kernel(pair, across, out):
    count = out.shape[0]
    out[...] = added(pair[:count, :], across[:count, :]).astype(jnp.bfloat16)


def small_call(kernel, rows, *args):
    vmem = pl.BlockSpec(memory_space=pltpu.VMEM)
    shape = (rows, args[0].shape[1])
    return pl.pallas_call(
        kernel,
        out_shape=jax.ShapeDtypeStruct(shape, jnp.bfloat16),
        in_specs=[vmem] * len(args),
        out_specs=vmem,
        compiler_params=pltpu.CompilerParams(vmem_limit_bytes=ROTATE_VMEM),
        cost_estimate=pl.CostEstimate(flops=rows * shape[1], bytes_accessed=8 * rows * shape[1], transcendentals=0),
    )(*args)


def outer_columns(first, flat, turned, g, eig, precond, score, ratio, outs):
    rows = ratio.shape[0] // outs.shape[0]
    where = pl.ds(pl.multiple_of(first, ratio.shape[1]), ratio.shape[1])
    stores = []
    for i in range(outs.shape[0]):
        block = slice(i * rows, (i + 1) * rows)
        outer = jnp.dot(turned[block, :], g[...], preferred_element_type=jnp.float32)
        ratio[block, :] = outer / eig[block, :]
        stores.append(pltpu.make_async_copy(ratio.at[block, :], precond.at[block, where], outs.at[i]))
        stores[-1].start()
    mapped = jnp.dot(flat[...], ratio[...].astype(jnp.bfloat16), preferred_element_type=jnp.float32)
    part = mapped * g[...].astype(jnp.float32)
    folded = score[...]
    for lane in range(0, part.shape[1], score.shape[1]):
        folded = folded + part[:, lane : lane + score.shape[1]]
    score[...] = folded
    for store in stores:
        store.wait()


def near_kernel(
    place, a0, a1, a2, a3, g, eig, precond, score, flat, turned, later, parts, grads, tile, ratio, outs, loads
):
    half = grads.shape[1]
    copies = [pltpu.make_async_copy(a, parts.at[m], loads.at[m]) for m, a in enumerate((a0, a1, a2, a3))]
    copies.append(pltpu.make_async_copy(g, grads, loads.at[4]))
    for i, kept in ((0, tile), (1, later)):
        where = pl.ds(pl.multiple_of(place[1 + i] * half, half), half)
        copies.append(pltpu.make_async_copy(eig.at[:, where], kept, loads.at[5 + i]))
    for copy in copies:
        copy.start()
    tok = parts.shape[1] // 4
    piece = parts.shape[2]
    for m in range(4):
        copies[m].wait()
        where = pl.ds(pl.multiple_of((place[0] ^ m) * piece, piece), piece)
        rows = jnp.concatenate([parts[m, (j ^ m) * tok : ((j ^ m) + 1) * tok, :] for j in range(4)])
        flat[:, where] = rows
        turned[where, :] = rows.T
    score[...] = jnp.zeros_like(score)
    copies[4].wait()
    copies[5].wait()
    outer_columns(
        place[1] * half, flat, turned, grads, tile, precond, score, ratio, outs
    )
    copies[6].wait()


def far_kernel(place, flat, turned, g, eig, done, before, token, precond, value, score, ratio, outs):
    score[...] = before[...]
    outer_columns(
        place[2] * g.shape[1], flat, turned, g, eig, precond, score, ratio, outs
    )
    tok = score.shape[0] // 4
    for j in range(4):
        value[j : j + 1, :] = jnp.sum(score[j * tok : (j + 1) * tok, :].T, axis=0, keepdims=True)


def finish_kernel(scale_score, scale_influence, parts, scores, influence):
    tok = scores.shape[0]
    scores[...] = jnp.sum(parts[:, :tok], axis=0) * scale_score
    influence[...] = jnp.sum(parts[:, tok:], axis=0) * scale_influence


def outer_near(place, acts, grads, eigvals):
    width = eigvals.shape[0]
    tokens, cols = grads.shape
    vmem, hbm = pl.BlockSpec(memory_space=pltpu.VMEM), pl.BlockSpec(memory_space=pltpu.HBM)
    anywhere = pl.BlockSpec(memory_space=pl.ANY)
    return pl.pallas_call(
        near_kernel,
        out_shape=(
            jax.ShapeDtypeStruct(eigvals.shape, jnp.float32),
            jax.ShapeDtypeStruct((tokens, LANES), jnp.float32),
            jax.ShapeDtypeStruct((tokens, width), jnp.bfloat16),
            jax.ShapeDtypeStruct((width, tokens), jnp.bfloat16),
            jax.ShapeDtypeStruct((width, cols), jnp.float32),
        ),
        in_specs=[pl.BlockSpec(memory_space=pltpu.SMEM)] + [anywhere] * 5 + [hbm],
        out_specs=(hbm, vmem, vmem, vmem, vmem),
        scratch_shapes=[
            pltpu.VMEM((4, tokens, width // 4), jnp.bfloat16),
            pltpu.VMEM((tokens, cols), jnp.bfloat16),
            pltpu.VMEM((width, cols), jnp.float32),
            pltpu.VMEM((width, cols), jnp.float32),
            pltpu.SemaphoreType.DMA((BLOCKS,)),
            pltpu.SemaphoreType.DMA((7,)),
        ],
        compiler_params=pltpu.CompilerParams(vmem_limit_bytes=NEAR_VMEM),
        cost_estimate=pl.CostEstimate(
            flops=4 * tokens * width * cols, bytes_accessed=12 * width * cols, transcendentals=0
        ),
        name="outer_near",
    )(place, *acts, grads, eigvals)


def outer_far(place, flat, turned, grads, eigvals, done, before, token):
    tokens, cols = grads.shape
    width = done.shape[0]
    vmem, hbm = pl.BlockSpec(memory_space=pltpu.VMEM), pl.BlockSpec(memory_space=pltpu.HBM)
    return pl.pallas_call(
        far_kernel,
        out_shape=(
            jax.ShapeDtypeStruct(done.shape, jnp.float32),
            jax.ShapeDtypeStruct((4, tokens // 4), jnp.float32),
        ),
        in_specs=[pl.BlockSpec(memory_space=pltpu.SMEM), vmem, vmem, vmem, vmem, hbm, vmem, vmem],
        out_specs=(hbm, vmem),
        scratch_shapes=[
            pltpu.VMEM((tokens, LANES), jnp.float32),
            pltpu.VMEM((width, cols), jnp.float32),
            pltpu.SemaphoreType.DMA((BLOCKS,)),
        ],
        input_output_aliases={5: 0},
        compiler_params=pltpu.CompilerParams(vmem_limit_bytes=VMEM),
        cost_estimate=pl.CostEstimate(
            flops=4 * tokens * width * cols, bytes_accessed=4 * width * cols, transcendentals=0
        ),
        name="outer_far",
    )(place, flat, turned, grads, eigvals, done, before, token)


def local_pairs(acts, grads, source_ids, basis_in, basis_out, eigvals):
    seqs, rows, cols = (lax.axis_size(name) for name in PLANE)
    s = lax.axis_index("seq")
    x = lax.axis_index("row")
    k = lax.axis_index("col")
    u = k * rows + x
    low, high = s % 2, s // 2
    tok = acts.shape[0]
    total_tokens = tok * seqs
    block = acts.shape[1]
    width = block * rows * cols
    half, piece = block // 2, block // 4

    def turned(x, flip):
        pairs = []
        for b in range(seqs):
            for f in range(rows * cols):
                pairs.append((b * rows * cols + f, ((f ^ flip) * rows + b % rows) * cols + b // rows))
        return lax.ppermute(x, PLANE, pairs)

    def plane_gather(x):
        near = swap(x, "row")
        return [x, near, swap(x, "col"), swap(near, "col")]

    tie = lambda *values: lax.optimization_barrier(values)
    token = jnp.zeros((8, LANES), jnp.float32)
    acts_there = swap(acts, "row")
    grads_here = turned(grads, 0)
    theirs = swap(jnp.where(k == 0, basis_in[:, half:], basis_in[:, :half]), "col")
    basis_out = jnp.concatenate(
        [lax.dynamic_slice_in_dim(basis_out, at * half, half, axis=1) for at in (1 - low, low)], axis=1
    )
    note = lambda *ids: jnp.concatenate([jnp.pad(jnp.stack(ids), ((0, 16 - len(ids)), (0, half - tok)))])
    source_ids = source_ids.astype(jnp.bfloat16)
    acts_here = turned(acts_there, cols)
    (token,) = stand(token)
    token, grads_here, basis_in, basis_out = tie(token, grads_here, basis_in, basis_out)
    grads_far = swap(grads_here, "row")
    mine = lax.dynamic_slice_in_dim(basis_in, k * half, half, axis=1)
    first, second = jnp.where(k == low, mine, theirs), jnp.where(k == low, theirs, mine)
    first, second = (jnp.roll(t, -(1 - x) * piece, axis=1) for t in (first, second))
    tiles = jnp.concatenate([second[:, piece:], second[:, :piece], first[:, :piece], first[:, piece:]], axis=1)
    (token,) = stand(token)
    token, grads_far, tiles, grads_here = tie(token, grads_far, tiles, grads_here)
    grads_both = swap(grads_far, "col")
    grads_near = swap(grads_here, "col")
    token, acts_here = tie(token, acts_here)
    send_g, keep_g = rotate([grads_here, grads_far, grads_near, grads_both], basis_out, 1, note(source_ids))
    got_g = swap(send_g, "seq", 1)
    acts_here, keep_g = tie(acts_here, keep_g)
    acts_far = swap(acts_here, "row")
    token, keep_g = stand(token, keep_g)
    token, acts_far, acts_here = tie(token, acts_far, acts_here)
    acts_both = swap(acts_far, "col")
    acts_near = swap(acts_here, "col")
    to_pair, to_both, to_x, keep_a = rotate([acts_here, acts_far, acts_near, acts_both], tiles, 3, flips=(1, 2))
    from_both = lax.ppermute(
        to_both,
        ("seq", "row"),
        [(i * rows + j, (i ^ 1) * rows + (j ^ 1)) for i in range(seqs) for j in range(rows)],
    )
    from_pair = swap(to_pair, "seq", 1)
    from_x = swap(to_x, "row")
    token, keep_a = tie(token, keep_a)
    token, got_g = tie(token, got_g)
    count = seqs * tok
    pair_g = small_call(pair_kernel, count + 16, keep_g, got_g, note(source_ids))
    token, pair_g = tie(token, pair_g)
    across_g = swap(pair_g, "seq", 2)
    (token,) = stand(token)
    token, from_x, from_pair, from_both = tie(token, from_x, from_pair, from_both)
    same, swapped = added(keep_a, from_pair), added(from_x, from_both)
    stay = jnp.where(x == high, same, swapped)
    cross = swap(jnp.where(x == high, swapped, same).astype(jnp.bfloat16), "seq", 2)
    token, across_g = tie(token, across_g)
    near_g = small_call(sum_kernel, count, pair_g, across_g)
    token, near_g = tie(token, near_g)
    far_g = swap(near_g, "seq", 1)
    (token,) = stand(token)
    token, cross = tie(token, cross)
    own_a = (stay + cross.astype(jnp.float32)).astype(jnp.bfloat16)
    quarters = plane_gather(own_a)

    ids = jnp.stack([source_ids, got_g[count, :tok], across_g[count, :tok], across_g[count + 1, :tok]])
    slot_ids = jnp.stack([lax.dynamic_index_in_dim(ids, u ^ s ^ j, keepdims=False) for j in range(seqs)])
    place = jnp.stack([u, low, 1 - low]).astype(jnp.int32)
    precond, value, flat, across, later = outer_near(place, quarters, near_g, eigvals)
    precond, slots = outer_far(place, flat, across, far_g, later, precond, value, token)
    chosen = slot_ids[None] == jnp.arange(SOURCES, dtype=jnp.bfloat16)[:, None, None]
    part = jnp.sum(jnp.where(chosen, slots[None], 0.0), axis=(1, 2))
    blocks = jnp.stack([lax.dynamic_index_in_dim(slots, u ^ j, keepdims=False) for j in range(seqs)])
    message = jnp.concatenate([blocks, jnp.broadcast_to(part[None, :], (seqs, SOURCES))], axis=1)
    message = jnp.broadcast_to(message[:, None, :], (seqs, rows * cols, tok + SOURCES))
    message = message.reshape(seqs * rows * cols, tok + SOURCES)
    parts = lax.all_to_all(message, PLANE, split_axis=0, concat_axis=0, tiled=True)
    scale_score = float(total_tokens) / float(width * width)
    vmem = pl.BlockSpec(memory_space=pltpu.VMEM)
    scores, influence = pl.pallas_call(
        functools.partial(finish_kernel, scale_score, scale_score * (float(SOURCES) / float(total_tokens))),
        out_shape=(jax.ShapeDtypeStruct((tok,), jnp.float32), jax.ShapeDtypeStruct((SOURCES,), jnp.float32)),
        in_specs=[vmem],
        out_specs=(vmem, vmem),
        compiler_params=pltpu.CompilerParams(vmem_limit_bytes=2**20),
        name="finish",
    )(parts)
    return (precond, scores, influence)


def solution(mesh):
    in_specs = (
        P(("grp", "seq"), ("row", "col")),
        P(("grp", "seq"), ("row", "col")),
        P(("grp", "seq")),
        P("seq", ("row", "col")),
        P("seq", ("row", "col")),
        P("seq", ("row", "col")),
    )
    out_specs = (P(("grp", "seq"), ("row", "col")), P(("grp", "seq")), P("grp"))
    fits = (mesh.shape["seq"], mesh.shape["row"], mesh.shape["col"]) == (4, 2, 2)
    local = local_pairs if fits else local_any
    return jax.shard_map(local, mesh=mesh, in_specs=in_specs, out_specs=out_specs, check_vma=False)
```

```python
import functools

import jax
import jax.numpy as jnp
from jax import lax
from jax.experimental import pallas as pl
from jax.experimental.pallas import tpu as pltpu
from jax.sharding import PartitionSpec as P

SOURCES = 8
PLANE = ("seq", "row", "col")


def turn(x, pairs):
    return lax.ppermute(x, PLANE, pairs)


def local_any(acts, grads, source_ids, basis_in, basis_out, eigvals):
    seqs, rows, cols = (lax.axis_size(name) for name in PLANE)
    s = lax.axis_index("seq")
    tok = acts.shape[0]
    total_tokens = tok * seqs
    width = acts.shape[1] * rows * cols
    u = lax.axis_index("col") * rows + lax.axis_index("row")

    def place(seq, block):
        return (seq * rows + block % rows) * cols + block // rows

    def device(seq, feature):
        return seq * rows * cols + feature

    def along(axis, size, step):
        return [(i, i ^ step) for i in range(size)]

    def plane_gather(x):
        held = [x] + [lax.ppermute(x, "row", along("row", rows, j)) for j in range(1, rows)]
        slots = list(held)
        for j in range(1, cols):
            slots += [lax.ppermute(h, "col", along("col", cols, j)) for h in held]
        return slots

    def turned(x):
        pairs = [(device(b, f), place(f, b)) for b in range(seqs) for f in range(rows * cols)]
        return plane_gather(turn(x, pairs))

    def rotate(slots, basis):
        whole = jnp.stack(slots)
        pieces = []
        for k in range(seqs):
            x = lax.dynamic_index_in_dim(whole, u ^ s ^ k, keepdims=False)
            pieces.append(jnp.dot(x, basis, preferred_element_type=jnp.float32).astype(jnp.bfloat16))
        return pieces

    def total(parts):
        out = parts[0].astype(jnp.float32)
        for part in parts[1:]:
            out = out + part.astype(jnp.float32)
        return out

    grad_slots = turned(grads)
    act_slots = turned(acts)
    ids = [source_ids] + [lax.ppermute(source_ids, "seq", along("seq", seqs, k)) for k in range(1, seqs)]

    grad_pieces = rotate(grad_slots, basis_out)
    got = [grad_pieces[0]] + [
        lax.ppermute(grad_pieces[k], "seq", along("seq", seqs, k)) for k in range(1, seqs)
    ]
    own_grads = total(got).astype(jnp.bfloat16)
    rg = [own_grads] + [lax.ppermute(own_grads, "seq", along("seq", seqs, k)) for k in range(1, seqs)]

    act_pieces = rotate(act_slots, basis_in)
    got = []
    for k in range(seqs):
        pairs = [(device(b, f), place(f, b ^ k)) for b in range(seqs) for f in range(rows * cols)]
        got.append(turn(act_pieces[k], pairs))
    own_acts = total(got).astype(jnp.bfloat16)
    whole = jnp.stack(plane_gather(own_acts))
    ra = [lax.dynamic_index_in_dim(whole, u ^ s ^ k, keepdims=False) for k in range(seqs)]

    outer = jnp.zeros(eigvals.shape, jnp.float32)
    for k in range(seqs):
        partial = lax.dot_general(
            ra[k], rg[k], (((0,), (0,)), ((), ())), preferred_element_type=jnp.float32
        )
        outer = outer + partial.astype(jnp.bfloat16).astype(jnp.float32)
    precond = outer / eigvals
    precond_rounded = precond.astype(jnp.bfloat16)
    all_ra, all_rg = jnp.concatenate(ra), jnp.concatenate(rg)
    mapped = lax.dot_general(
        all_rg, precond_rounded, (((1,), (1,)), ((), ())), preferred_element_type=jnp.float32
    )
    partial_value = jnp.sum(mapped * all_ra.astype(jnp.float32), axis=1)
    near = partial_value
    for axis, size in (("col", cols), ("row", rows)):
        near = total([near] + [lax.ppermute(near, axis, along(axis, size, j)) for j in range(1, size)])
    all_ids = jnp.concatenate(ids)
    onehot = (all_ids[:, None] == jnp.arange(SOURCES, dtype=jnp.int32)[None, :]).astype(jnp.float32)
    near_influence = jnp.sum(onehot * near[:, None], axis=0)
    blocks = near.reshape(seqs, tok)
    far = [jnp.concatenate([blocks[k], near_influence]) for k in range(seqs)]
    summed = total([far[0]] + [lax.ppermute(far[k], "seq", along("seq", seqs, k)) for k in range(1, seqs)])
    scale_score = float(total_tokens) / float(width * width)
    scores = summed[:tok] * scale_score
    influence = summed[tok:] * (scale_score * (float(SOURCES) / float(total_tokens)))
    return (precond, scores, influence)


VMEM = 16 * 2**20
NEAR_VMEM = 48 * 2**20
ROTATE_VMEM = 10 * 2**20
LANES = 128
STAND = 2 * 10**10
BLOCKS = 4


def swap(x, axis, step=1):
    return lax.ppermute(x, axis, [(i, i ^ step) for i in range(lax.axis_size(axis))])


def stand_kernel(x, out):
    out[...] = x[...]


def stand(token, *values):
    token, *values = lax.optimization_barrier((token, *values))
    vmem = pl.BlockSpec(memory_space=pltpu.VMEM)
    token = pl.pallas_call(
        stand_kernel,
        out_shape=jax.ShapeDtypeStruct(token.shape, token.dtype),
        in_specs=[vmem],
        out_specs=vmem,
        compiler_params=pltpu.CompilerParams(vmem_limit_bytes=2**20),
        cost_estimate=pl.CostEstimate(flops=STAND, bytes_accessed=0, transcendentals=0),
        name="stand",
    )(token)
    return token, *values


def added(a, b):
    return a.astype(jnp.float32) + b.astype(jnp.float32)


def rotate_kernel(x0, x1, x2, x3, basis, *refs, notes, flips):
    note, (*sends, keep, rows) = refs[:notes], refs[notes:]
    tok = x0.shape[0]
    for j, x in enumerate((x0, x1, x2, x3)):
        rows[pl.ds(j * tok, tok), :] = x[...]
    at = 0
    for i, out in enumerate((*sends, keep)):
        cut = out.shape[1]
        block = jnp.dot(rows[...], basis[:, at : at + cut], preferred_element_type=jnp.float32)
        for j in range(4):
            k = j ^ (i in flips)
            out[j * tok : (j + 1) * tok, :] = block[k * tok : (k + 1) * tok, :].astype(out.dtype)
        at += cut
    if note:
        sends[0][rows.shape[0] :, :] = note[0][...]


def rotate(slots, basis, messages, *note, flips=()):
    tok, depth = slots[0].shape
    rows, cols = tok * len(slots), basis.shape[1]
    cut = cols // (messages + 1)
    vmem = pl.BlockSpec(memory_space=pltpu.VMEM)
    return pl.pallas_call(
        functools.partial(rotate_kernel, notes=len(note), flips=flips),
        out_shape=[jax.ShapeDtypeStruct((rows + sum(n.shape[0] for n in note), cut), jnp.bfloat16)] * messages
        + [jax.ShapeDtypeStruct((rows, cut), jnp.float32)],
        in_specs=[vmem] * (5 + len(note)),
        out_specs=[vmem] * (messages + 1),
        scratch_shapes=[pltpu.VMEM((rows, depth), jnp.bfloat16)],
        compiler_params=pltpu.CompilerParams(vmem_limit_bytes=ROTATE_VMEM),
        cost_estimate=pl.CostEstimate(flops=2 * rows * depth * cols, bytes_accessed=2 * depth * cols, transcendentals=0),
        name="rotate",
    )(*slots, basis, *note)


def pair_kernel(keep, got, note, out):
    count = keep.shape[0]
    out[:count, :] = (keep[...] + got[:count, :].astype(jnp.float32)).astype(jnp.bfloat16)
    row = lax.broadcasted_iota(jnp.int32, note.shape, 0)
    theirs = jnp.broadcast_to(got[count:, :].astype(jnp.float32)[:1], note.shape)
    out[count:, :] = jnp.where(row == 1, theirs, note[...].astype(jnp.float32)).astype(jnp.bfloat16)


def sum_kernel(pair, across, out):
    count = out.shape[0]
    out[...] = added(pair[:count, :], across[:count, :]).astype(jnp.bfloat16)


def small_call(kernel, rows, *args):
    vmem = pl.BlockSpec(memory_space=pltpu.VMEM)
    shape = (rows, args[0].shape[1])
    return pl.pallas_call(
        kernel,
        out_shape=jax.ShapeDtypeStruct(shape, jnp.bfloat16),
        in_specs=[vmem] * len(args),
        out_specs=vmem,
        compiler_params=pltpu.CompilerParams(vmem_limit_bytes=ROTATE_VMEM),
        cost_estimate=pl.CostEstimate(flops=rows * shape[1], bytes_accessed=8 * rows * shape[1], transcendentals=0),
    )(*args)


def outer_columns(first, flat, turned, g, eig, precond, score, ratio, outs):
    rows = ratio.shape[0] // outs.shape[0]
    where = pl.ds(pl.multiple_of(first, ratio.shape[1]), ratio.shape[1])
    stores = []
    for i in range(outs.shape[0]):
        block = slice(i * rows, (i + 1) * rows)
        outer = jnp.dot(turned[block, :], g[...], preferred_element_type=jnp.float32)
        ratio[block, :] = outer / eig[block, :]
        stores.append(pltpu.make_async_copy(ratio.at[block, :], precond.at[block, where], outs.at[i]))
        stores[-1].start()
    mapped = jnp.dot(flat[...], ratio[...].astype(jnp.bfloat16), preferred_element_type=jnp.float32)
    part = mapped * g[...].astype(jnp.float32)
    folded = score[...]
    for lane in range(0, part.shape[1], score.shape[1]):
        folded = folded + part[:, lane : lane + score.shape[1]]
    score[...] = folded
    for store in stores:
        store.wait()


def near_kernel(
    place, a0, a1, a2, a3, g, eig, precond, score, flat, turned, later, parts, grads, tile, ratio, outs, loads
):
    half = grads.shape[1]
    copies = [pltpu.make_async_copy(a, parts.at[m], loads.at[m]) for m, a in enumerate((a0, a1, a2, a3))]
    copies.append(pltpu.make_async_copy(g, grads, loads.at[4]))
    for i, kept in ((0, tile), (1, later)):
        where = pl.ds(pl.multiple_of(place[1 + i] * half, half), half)
        copies.append(pltpu.make_async_copy(eig.at[:, where], kept, loads.at[5 + i]))
    for copy in copies:
        copy.start()
    tok = parts.shape[1] // 4
    piece = parts.shape[2]
    for m in range(4):
        copies[m].wait()
        where = pl.ds(pl.multiple_of((place[0] ^ m) * piece, piece), piece)
        rows = jnp.concatenate([parts[m, (j ^ m) * tok : ((j ^ m) + 1) * tok, :] for j in range(4)])
        flat[:, where] = rows
        turned[where, :] = rows.T
    score[...] = jnp.zeros_like(score)
    copies[4].wait()
    copies[5].wait()
    outer_columns(
        place[1] * half, flat, turned, grads, tile, precond, score, ratio, outs
    )
    copies[6].wait()


def far_kernel(place, flat, turned, g, eig, done, before, token, precond, value, score, ratio, outs):
    score[...] = before[...]
    outer_columns(
        place[2] * g.shape[1], flat, turned, g, eig, precond, score, ratio, outs
    )
    tok = score.shape[0] // 4
    for j in range(4):
        value[j : j + 1, :] = jnp.sum(score[j * tok : (j + 1) * tok, :].T, axis=0, keepdims=True)


def finish_kernel(scale_score, scale_influence, parts, scores, influence):
    tok = scores.shape[0]
    scores[...] = jnp.sum(parts[:, :tok], axis=0) * scale_score
    influence[...] = jnp.sum(parts[:, tok : tok + SOURCES], axis=0) * scale_influence


def outer_near(place, acts, grads, eigvals):
    width = eigvals.shape[0]
    tokens, cols = grads.shape
    vmem, hbm = pl.BlockSpec(memory_space=pltpu.VMEM), pl.BlockSpec(memory_space=pltpu.HBM)
    anywhere = pl.BlockSpec(memory_space=pl.ANY)
    return pl.pallas_call(
        near_kernel,
        out_shape=(
            jax.ShapeDtypeStruct(eigvals.shape, jnp.float32),
            jax.ShapeDtypeStruct((tokens, LANES), jnp.float32),
            jax.ShapeDtypeStruct((tokens, width), jnp.bfloat16),
            jax.ShapeDtypeStruct((width, tokens), jnp.bfloat16),
            jax.ShapeDtypeStruct((width, cols), jnp.float32),
        ),
        in_specs=[pl.BlockSpec(memory_space=pltpu.SMEM)] + [anywhere] * 5 + [hbm],
        out_specs=(hbm, vmem, vmem, vmem, vmem),
        scratch_shapes=[
            pltpu.VMEM((4, tokens, width // 4), jnp.bfloat16),
            pltpu.VMEM((tokens, cols), jnp.bfloat16),
            pltpu.VMEM((width, cols), jnp.float32),
            pltpu.VMEM((width, cols), jnp.float32),
            pltpu.SemaphoreType.DMA((BLOCKS,)),
            pltpu.SemaphoreType.DMA((7,)),
        ],
        compiler_params=pltpu.CompilerParams(vmem_limit_bytes=NEAR_VMEM),
        cost_estimate=pl.CostEstimate(
            flops=4 * tokens * width * cols, bytes_accessed=12 * width * cols, transcendentals=0
        ),
        name="outer_near",
    )(place, *acts, grads, eigvals)


def outer_far(place, flat, turned, grads, eigvals, done, before, token):
    tokens, cols = grads.shape
    width = done.shape[0]
    vmem, hbm = pl.BlockSpec(memory_space=pltpu.VMEM), pl.BlockSpec(memory_space=pltpu.HBM)
    return pl.pallas_call(
        far_kernel,
        out_shape=(
            jax.ShapeDtypeStruct(done.shape, jnp.float32),
            jax.ShapeDtypeStruct((4, tokens // 4), jnp.float32),
        ),
        in_specs=[pl.BlockSpec(memory_space=pltpu.SMEM), vmem, vmem, vmem, vmem, hbm, vmem, vmem],
        out_specs=(hbm, vmem),
        scratch_shapes=[
            pltpu.VMEM((tokens, LANES), jnp.float32),
            pltpu.VMEM((width, cols), jnp.float32),
            pltpu.SemaphoreType.DMA((BLOCKS,)),
        ],
        input_output_aliases={5: 0},
        compiler_params=pltpu.CompilerParams(vmem_limit_bytes=VMEM),
        cost_estimate=pl.CostEstimate(
            flops=4 * tokens * width * cols, bytes_accessed=4 * width * cols, transcendentals=0
        ),
        name="outer_far",
    )(place, flat, turned, grads, eigvals, done, before, token)


def local_pairs(acts, grads, source_ids, basis_in, basis_out, eigvals):
    seqs, rows, cols = (lax.axis_size(name) for name in PLANE)
    s = lax.axis_index("seq")
    x = lax.axis_index("row")
    k = lax.axis_index("col")
    u = k * rows + x
    low, high = s % 2, s // 2
    tok = acts.shape[0]
    total_tokens = tok * seqs
    block = acts.shape[1]
    width = block * rows * cols
    half, piece = block // 2, block // 4

    def turned(x, flip):
        pairs = []
        for b in range(seqs):
            for f in range(rows * cols):
                pairs.append((b * rows * cols + f, ((f ^ flip) * rows + b % rows) * cols + b // rows))
        return lax.ppermute(x, PLANE, pairs)

    def plane_gather(x):
        near = swap(x, "row")
        return [x, near, swap(x, "col"), swap(near, "col")]

    tie = lambda *values: lax.optimization_barrier(values)
    token = jnp.zeros((8, LANES), jnp.float32)
    acts_there = swap(acts, "row")
    grads_here = turned(grads, 0)
    theirs = swap(jnp.where(k == 0, basis_in[:, half:], basis_in[:, :half]), "col")
    basis_out = jnp.concatenate(
        [lax.dynamic_slice_in_dim(basis_out, at * half, half, axis=1) for at in (1 - low, low)], axis=1
    )
    note = lambda *ids: jnp.concatenate([jnp.pad(jnp.stack(ids), ((0, 16 - len(ids)), (0, half - tok)))])
    source_ids = source_ids.astype(jnp.bfloat16)
    acts_here = turned(acts_there, cols)
    (token,) = stand(token)
    token, grads_here, basis_in, basis_out = tie(token, grads_here, basis_in, basis_out)
    grads_far = swap(grads_here, "row")
    mine = lax.dynamic_slice_in_dim(basis_in, k * half, half, axis=1)
    first, second = jnp.where(k == low, mine, theirs), jnp.where(k == low, theirs, mine)
    first, second = (jnp.roll(t, -(1 - x) * piece, axis=1) for t in (first, second))
    tiles = jnp.concatenate([second[:, piece:], second[:, :piece], first[:, :piece], first[:, piece:]], axis=1)
    (token,) = stand(token)
    token, grads_far, tiles, grads_here = tie(token, grads_far, tiles, grads_here)
    grads_both = swap(grads_far, "col")
    grads_near = swap(grads_here, "col")
    token, acts_here = tie(token, acts_here)
    send_g, keep_g = rotate([grads_here, grads_far, grads_near, grads_both], basis_out, 1, note(source_ids))
    got_g = swap(send_g, "seq", 1)
    acts_here, keep_g = tie(acts_here, keep_g)
    acts_far = swap(acts_here, "row")
    token, keep_g = tie(token, keep_g)
    token, acts_far, acts_here = tie(token, acts_far, acts_here)
    acts_both = swap(acts_far, "col")
    acts_near = swap(acts_here, "col")
    to_pair, to_both, to_x, keep_a = rotate([acts_here, acts_far, acts_near, acts_both], tiles, 3, flips=(1, 2))
    from_both = lax.ppermute(
        to_both,
        ("seq", "row"),
        [(i * rows + j, (i ^ 1) * rows + (j ^ 1)) for i in range(seqs) for j in range(rows)],
    )
    from_pair = swap(to_pair, "seq", 1)
    from_x = swap(to_x, "row")
    token, keep_a = tie(token, keep_a)
    token, got_g = tie(token, got_g)
    count = seqs * tok
    pair_g = small_call(pair_kernel, count + 16, keep_g, got_g, note(source_ids))
    token, pair_g = tie(token, pair_g)
    across_g = swap(pair_g, "seq", 2)
    (token,) = stand(token)
    token, from_x, from_pair, from_both = tie(token, from_x, from_pair, from_both)
    same, swapped = added(keep_a, from_pair), added(from_x, from_both)
    stay = jnp.where(x == high, same, swapped)
    cross = swap(jnp.where(x == high, swapped, same).astype(jnp.bfloat16), "seq", 2)
    token, across_g = tie(token, across_g)
    near_g = small_call(sum_kernel, count, pair_g, across_g)
    token, near_g = tie(token, near_g)
    far_g = swap(near_g, "seq", 1)
    token, cross = tie(token, cross)
    own_a = (stay + cross.astype(jnp.float32)).astype(jnp.bfloat16)
    quarters = plane_gather(own_a)

    ids = jnp.stack([source_ids, got_g[count, :tok], across_g[count, :tok], across_g[count + 1, :tok]])
    slot_ids = jnp.stack([lax.dynamic_index_in_dim(ids, u ^ s ^ j, keepdims=False) for j in range(seqs)])
    place = jnp.stack([u, low, 1 - low]).astype(jnp.int32)
    precond, value, flat, across, later = outer_near(place, quarters, near_g, eigvals)
    precond, slots = outer_far(place, flat, across, far_g, later, precond, value, token)
    chosen = slot_ids[None] == jnp.arange(SOURCES, dtype=jnp.bfloat16)[:, None, None]
    part = jnp.sum(jnp.where(chosen, slots[None], 0.0), axis=(1, 2))
    blocks = jnp.stack([lax.dynamic_index_in_dim(slots, u ^ j, keepdims=False) for j in range(seqs)])
    message = jnp.concatenate([blocks, jnp.broadcast_to(part[None, :], (seqs, SOURCES))], axis=1)
    message = jnp.pad(message, ((0, 0), (0, tok - SOURCES)))
    message = jnp.broadcast_to(message[:, None, :], (seqs, rows * cols, 2 * tok))
    message = message.reshape(seqs * rows * cols, 2 * tok)
    parts = lax.all_to_all(message, PLANE, split_axis=0, concat_axis=0, tiled=True)
    scale_score = float(total_tokens) / float(width * width)
    vmem = pl.BlockSpec(memory_space=pltpu.VMEM)
    scores, influence = pl.pallas_call(
        functools.partial(finish_kernel, scale_score, scale_score * (float(SOURCES) / float(total_tokens))),
        out_shape=(jax.ShapeDtypeStruct((tok,), jnp.float32), jax.ShapeDtypeStruct((SOURCES,), jnp.float32)),
        in_specs=[vmem],
        out_specs=(vmem, vmem),
        compiler_params=pltpu.CompilerParams(vmem_limit_bytes=2**20),
        name="finish",
    )(parts)
    return (precond, scores, influence)


def solution(mesh):
    in_specs = (
        P(("grp", "seq"), ("row", "col")),
        P(("grp", "seq"), ("row", "col")),
        P(("grp", "seq")),
        P("seq", ("row", "col")),
        P("seq", ("row", "col")),
        P("seq", ("row", "col")),
    )
    out_specs = (P(("grp", "seq"), ("row", "col")), P(("grp", "seq")), P("grp"))
    fits = (mesh.shape["seq"], mesh.shape["row"], mesh.shape["col"]) == (4, 2, 2)
    local = local_pairs if fits else local_any
    return jax.shard_map(local, mesh=mesh, in_specs=in_specs, out_specs=out_specs, check_vma=False)
```

```python
import functools

import jax
import jax.numpy as jnp
from jax import lax
from jax.experimental import pallas as pl
from jax.experimental.pallas import tpu as pltpu
from jax.sharding import PartitionSpec as P

SOURCES = 8
PLANE = ("seq", "row", "col")


def turn(x, pairs):
    return lax.ppermute(x, PLANE, pairs)


def local_any(acts, grads, source_ids, basis_in, basis_out, eigvals):
    seqs, rows, cols = (lax.axis_size(name) for name in PLANE)
    s = lax.axis_index("seq")
    tok = acts.shape[0]
    total_tokens = tok * seqs
    width = acts.shape[1] * rows * cols
    u = lax.axis_index("col") * rows + lax.axis_index("row")

    def place(seq, block):
        return (seq * rows + block % rows) * cols + block // rows

    def device(seq, feature):
        return seq * rows * cols + feature

    def along(axis, size, step):
        return [(i, i ^ step) for i in range(size)]

    def plane_gather(x):
        held = [x] + [lax.ppermute(x, "row", along("row", rows, j)) for j in range(1, rows)]
        slots = list(held)
        for j in range(1, cols):
            slots += [lax.ppermute(h, "col", along("col", cols, j)) for h in held]
        return slots

    def turned(x):
        pairs = [(device(b, f), place(f, b)) for b in range(seqs) for f in range(rows * cols)]
        return plane_gather(turn(x, pairs))

    def rotate(slots, basis):
        whole = jnp.stack(slots)
        pieces = []
        for k in range(seqs):
            x = lax.dynamic_index_in_dim(whole, u ^ s ^ k, keepdims=False)
            pieces.append(jnp.dot(x, basis, preferred_element_type=jnp.float32).astype(jnp.bfloat16))
        return pieces

    def total(parts):
        out = parts[0].astype(jnp.float32)
        for part in parts[1:]:
            out = out + part.astype(jnp.float32)
        return out

    grad_slots = turned(grads)
    act_slots = turned(acts)
    ids = [source_ids] + [lax.ppermute(source_ids, "seq", along("seq", seqs, k)) for k in range(1, seqs)]

    grad_pieces = rotate(grad_slots, basis_out)
    got = [grad_pieces[0]] + [
        lax.ppermute(grad_pieces[k], "seq", along("seq", seqs, k)) for k in range(1, seqs)
    ]
    own_grads = total(got).astype(jnp.bfloat16)
    rg = [own_grads] + [lax.ppermute(own_grads, "seq", along("seq", seqs, k)) for k in range(1, seqs)]

    act_pieces = rotate(act_slots, basis_in)
    got = []
    for k in range(seqs):
        pairs = [(device(b, f), place(f, b ^ k)) for b in range(seqs) for f in range(rows * cols)]
        got.append(turn(act_pieces[k], pairs))
    own_acts = total(got).astype(jnp.bfloat16)
    whole = jnp.stack(plane_gather(own_acts))
    ra = [lax.dynamic_index_in_dim(whole, u ^ s ^ k, keepdims=False) for k in range(seqs)]

    outer = jnp.zeros(eigvals.shape, jnp.float32)
    for k in range(seqs):
        partial = lax.dot_general(
            ra[k], rg[k], (((0,), (0,)), ((), ())), preferred_element_type=jnp.float32
        )
        outer = outer + partial.astype(jnp.bfloat16).astype(jnp.float32)
    precond = outer / eigvals
    precond_rounded = precond.astype(jnp.bfloat16)
    all_ra, all_rg = jnp.concatenate(ra), jnp.concatenate(rg)
    mapped = lax.dot_general(
        all_rg, precond_rounded, (((1,), (1,)), ((), ())), preferred_element_type=jnp.float32
    )
    partial_value = jnp.sum(mapped * all_ra.astype(jnp.float32), axis=1)
    near = partial_value
    for axis, size in (("col", cols), ("row", rows)):
        near = total([near] + [lax.ppermute(near, axis, along(axis, size, j)) for j in range(1, size)])
    all_ids = jnp.concatenate(ids)
    onehot = (all_ids[:, None] == jnp.arange(SOURCES, dtype=jnp.int32)[None, :]).astype(jnp.float32)
    near_influence = jnp.sum(onehot * near[:, None], axis=0)
    blocks = near.reshape(seqs, tok)
    far = [jnp.concatenate([blocks[k], near_influence]) for k in range(seqs)]
    summed = total([far[0]] + [lax.ppermute(far[k], "seq", along("seq", seqs, k)) for k in range(1, seqs)])
    scale_score = float(total_tokens) / float(width * width)
    scores = summed[:tok] * scale_score
    influence = summed[tok:] * (scale_score * (float(SOURCES) / float(total_tokens)))
    return (precond, scores, influence)


VMEM = 16 * 2**20
NEAR_VMEM = 48 * 2**20
ROTATE_VMEM = 10 * 2**20
LANES = 128
STAND = 2 * 10**10
BLOCKS = 4


def swap(x, axis, step=1):
    return lax.ppermute(x, axis, [(i, i ^ step) for i in range(lax.axis_size(axis))])


def stand_kernel(x, out):
    out[...] = x[...]


def stand(token, *values):
    token, *values = lax.optimization_barrier((token, *values))
    vmem = pl.BlockSpec(memory_space=pltpu.VMEM)
    token = pl.pallas_call(
        stand_kernel,
        out_shape=jax.ShapeDtypeStruct(token.shape, token.dtype),
        in_specs=[vmem],
        out_specs=vmem,
        compiler_params=pltpu.CompilerParams(vmem_limit_bytes=2**20),
        cost_estimate=pl.CostEstimate(flops=STAND, bytes_accessed=0, transcendentals=0),
        name="stand",
    )(token)
    return token, *values


def added(a, b):
    return a.astype(jnp.float32) + b.astype(jnp.float32)


def rotate_kernel(x0, x1, x2, x3, basis, *refs, notes, flips):
    note, (*sends, keep, rows) = refs[:notes], refs[notes:]
    tok = x0.shape[0]
    for j, x in enumerate((x0, x1, x2, x3)):
        rows[pl.ds(j * tok, tok), :] = x[...]
    at = 0
    for i, out in enumerate((*sends, keep)):
        cut = out.shape[1]
        block = jnp.dot(rows[...], basis[:, at : at + cut], preferred_element_type=jnp.float32)
        for j in range(4):
            k = j ^ (i in flips)
            out[j * tok : (j + 1) * tok, :] = block[k * tok : (k + 1) * tok, :].astype(out.dtype)
        at += cut
    if note:
        sends[0][rows.shape[0] :, :] = note[0][...]


def rotate(slots, basis, messages, *note, flips=()):
    tok, depth = slots[0].shape
    rows, cols = tok * len(slots), basis.shape[1]
    cut = cols // (messages + 1)
    vmem = pl.BlockSpec(memory_space=pltpu.VMEM)
    return pl.pallas_call(
        functools.partial(rotate_kernel, notes=len(note), flips=flips),
        out_shape=[jax.ShapeDtypeStruct((rows + sum(n.shape[0] for n in note), cut), jnp.bfloat16)] * messages
        + [jax.ShapeDtypeStruct((rows, cut), jnp.float32)],
        in_specs=[vmem] * (5 + len(note)),
        out_specs=[vmem] * (messages + 1),
        scratch_shapes=[pltpu.VMEM((rows, depth), jnp.bfloat16)],
        compiler_params=pltpu.CompilerParams(vmem_limit_bytes=ROTATE_VMEM),
        cost_estimate=pl.CostEstimate(flops=2 * rows * depth * cols, bytes_accessed=2 * depth * cols, transcendentals=0),
        name="rotate",
    )(*slots, basis, *note)


def pair_kernel(keep, got, note, out):
    count = keep.shape[0]
    out[:count, :] = (keep[...] + got[:count, :].astype(jnp.float32)).astype(jnp.bfloat16)
    row = lax.broadcasted_iota(jnp.int32, note.shape, 0)
    theirs = jnp.broadcast_to(got[count:, :].astype(jnp.float32)[:1], note.shape)
    out[count:, :] = jnp.where(row == 1, theirs, note[...].astype(jnp.float32)).astype(jnp.bfloat16)


def sum_kernel(pair, across, out):
    count = out.shape[0]
    out[...] = added(pair[:count, :], across[:count, :]).astype(jnp.bfloat16)


def small_call(kernel, rows, *args):
    vmem = pl.BlockSpec(memory_space=pltpu.VMEM)
    shape = (rows, args[0].shape[1])
    return pl.pallas_call(
        kernel,
        out_shape=jax.ShapeDtypeStruct(shape, jnp.bfloat16),
        in_specs=[vmem] * len(args),
        out_specs=vmem,
        compiler_params=pltpu.CompilerParams(vmem_limit_bytes=ROTATE_VMEM),
        cost_estimate=pl.CostEstimate(flops=rows * shape[1], bytes_accessed=8 * rows * shape[1], transcendentals=0),
    )(*args)


def outer_columns(first, flat, turned, g, eig, precond, score, ratio, outs):
    rows = ratio.shape[0] // outs.shape[0]
    where = pl.ds(pl.multiple_of(first, ratio.shape[1]), ratio.shape[1])
    stores = []
    for i in range(outs.shape[0]):
        block = slice(i * rows, (i + 1) * rows)
        outer = jnp.dot(turned[block, :], g[...], preferred_element_type=jnp.float32)
        ratio[block, :] = outer / eig[block, :]
        stores.append(pltpu.make_async_copy(ratio.at[block, :], precond.at[block, where], outs.at[i]))
        stores[-1].start()
    mapped = jnp.dot(flat[...], ratio[...].astype(jnp.bfloat16), preferred_element_type=jnp.float32)
    part = mapped * g[...].astype(jnp.float32)
    folded = score[...]
    for lane in range(0, part.shape[1], score.shape[1]):
        folded = folded + part[:, lane : lane + score.shape[1]]
    score[...] = folded
    for store in stores:
        store.wait()


def near_kernel(
    place, a0, a1, a2, a3, g, eig, precond, score, flat, turned, later, parts, grads, tile, ratio, outs, loads
):
    half = grads.shape[1]
    copies = [pltpu.make_async_copy(a, parts.at[m], loads.at[m]) for m, a in enumerate((a0, a1, a2, a3))]
    copies.append(pltpu.make_async_copy(g, grads, loads.at[4]))
    for i, kept in ((0, tile), (1, later)):
        where = pl.ds(pl.multiple_of(place[1 + i] * half, half), half)
        copies.append(pltpu.make_async_copy(eig.at[:, where], kept, loads.at[5 + i]))
    for copy in copies:
        copy.start()
    tok = parts.shape[1] // 4
    piece = parts.shape[2]
    for m in range(4):
        copies[m].wait()
        where = pl.ds(pl.multiple_of((place[0] ^ m) * piece, piece), piece)
        rows = jnp.concatenate([parts[m, (j ^ m) * tok : ((j ^ m) + 1) * tok, :] for j in range(4)])
        flat[:, where] = rows
        turned[where, :] = rows.T
    score[...] = jnp.zeros_like(score)
    copies[4].wait()
    copies[5].wait()
    outer_columns(
        place[1] * half, flat, turned, grads, tile, precond, score, ratio, outs
    )
    copies[6].wait()


def far_kernel(place, flat, turned, g, eig, done, before, token, precond, value, score, ratio, outs):
    score[...] = before[...]
    outer_columns(
        place[2] * g.shape[1], flat, turned, g, eig, precond, score, ratio, outs
    )
    tok = score.shape[0] // 4
    for j in range(4):
        value[j : j + 1, :] = jnp.sum(score[j * tok : (j + 1) * tok, :].T, axis=0, keepdims=True)


def finish_kernel(scale_score, scale_influence, parts, scores, influence):
    tok = scores.shape[0]
    scores[...] = jnp.sum(parts[:, :tok], axis=0) * scale_score
    influence[...] = jnp.sum(parts[:, tok:], axis=0) * scale_influence


def outer_near(place, acts, grads, eigvals):
    width = eigvals.shape[0]
    tokens, cols = grads.shape
    vmem, hbm = pl.BlockSpec(memory_space=pltpu.VMEM), pl.BlockSpec(memory_space=pltpu.HBM)
    anywhere = pl.BlockSpec(memory_space=pl.ANY)
    return pl.pallas_call(
        near_kernel,
        out_shape=(
            jax.ShapeDtypeStruct(eigvals.shape, jnp.float32),
            jax.ShapeDtypeStruct((tokens, LANES), jnp.float32),
            jax.ShapeDtypeStruct((tokens, width), jnp.bfloat16),
            jax.ShapeDtypeStruct((width, tokens), jnp.bfloat16),
            jax.ShapeDtypeStruct((width, cols), jnp.float32),
        ),
        in_specs=[pl.BlockSpec(memory_space=pltpu.SMEM)] + [anywhere] * 5 + [hbm],
        out_specs=(hbm, vmem, vmem, vmem, vmem),
        scratch_shapes=[
            pltpu.VMEM((4, tokens, width // 4), jnp.bfloat16),
            pltpu.VMEM((tokens, cols), jnp.bfloat16),
            pltpu.VMEM((width, cols), jnp.float32),
            pltpu.VMEM((width, cols), jnp.float32),
            pltpu.SemaphoreType.DMA((BLOCKS,)),
            pltpu.SemaphoreType.DMA((7,)),
        ],
        compiler_params=pltpu.CompilerParams(vmem_limit_bytes=NEAR_VMEM),
        cost_estimate=pl.CostEstimate(
            flops=4 * tokens * width * cols, bytes_accessed=12 * width * cols, transcendentals=0
        ),
        name="outer_near",
    )(place, *acts, grads, eigvals)


def outer_far(place, flat, turned, grads, eigvals, done, before, token):
    tokens, cols = grads.shape
    width = done.shape[0]
    vmem, hbm = pl.BlockSpec(memory_space=pltpu.VMEM), pl.BlockSpec(memory_space=pltpu.HBM)
    return pl.pallas_call(
        far_kernel,
        out_shape=(
            jax.ShapeDtypeStruct(done.shape, jnp.float32),
            jax.ShapeDtypeStruct((4, tokens // 4), jnp.float32),
        ),
        in_specs=[pl.BlockSpec(memory_space=pltpu.SMEM), vmem, vmem, vmem, vmem, hbm, vmem, vmem],
        out_specs=(hbm, vmem),
        scratch_shapes=[
            pltpu.VMEM((tokens, LANES), jnp.float32),
            pltpu.VMEM((width, cols), jnp.float32),
            pltpu.SemaphoreType.DMA((BLOCKS,)),
        ],
        input_output_aliases={5: 0},
        compiler_params=pltpu.CompilerParams(vmem_limit_bytes=VMEM),
        cost_estimate=pl.CostEstimate(
            flops=4 * tokens * width * cols, bytes_accessed=4 * width * cols, transcendentals=0
        ),
        name="outer_far",
    )(place, flat, turned, grads, eigvals, done, before, token)


def local_pairs(acts, grads, source_ids, basis_in, basis_out, eigvals):
    seqs, rows, cols = (lax.axis_size(name) for name in PLANE)
    s = lax.axis_index("seq")
    x = lax.axis_index("row")
    k = lax.axis_index("col")
    u = k * rows + x
    low, high = s % 2, s // 2
    tok = acts.shape[0]
    total_tokens = tok * seqs
    block = acts.shape[1]
    width = block * rows * cols
    half, piece = block // 2, block // 4

    def turned(x, flip):
        pairs = []
        for b in range(seqs):
            for f in range(rows * cols):
                pairs.append((b * rows * cols + f, ((f ^ flip) * rows + b % rows) * cols + b // rows))
        return lax.ppermute(x, PLANE, pairs)

    def plane_gather(x):
        near = swap(x, "row")
        return [x, near, swap(x, "col"), swap(near, "col")]

    tie = lambda *values: lax.optimization_barrier(values)
    token = jnp.zeros((8, LANES), jnp.float32)
    acts_there = swap(acts, "row")
    grads_here = turned(grads, 0)
    theirs = swap(jnp.where(k == 0, basis_in[:, half:], basis_in[:, :half]), "col")
    basis_out = jnp.concatenate(
        [lax.dynamic_slice_in_dim(basis_out, at * half, half, axis=1) for at in (1 - low, low)], axis=1
    )
    note = lambda *ids: jnp.concatenate([jnp.pad(jnp.stack(ids), ((0, 16 - len(ids)), (0, half - tok)))])
    source_ids = source_ids.astype(jnp.bfloat16)
    acts_here = turned(acts_there, cols)
    (token,) = stand(token)
    token, grads_here, basis_in, basis_out = tie(token, grads_here, basis_in, basis_out)
    grads_far = swap(grads_here, "row")
    mine = lax.dynamic_slice_in_dim(basis_in, k * half, half, axis=1)
    first, second = jnp.where(k == low, mine, theirs), jnp.where(k == low, theirs, mine)
    first, second = (jnp.roll(t, -(1 - x) * piece, axis=1) for t in (first, second))
    tiles = jnp.concatenate([second[:, piece:], second[:, :piece], first[:, :piece], first[:, piece:]], axis=1)
    (token,) = stand(token)
    token, grads_far, tiles, grads_here = tie(token, grads_far, tiles, grads_here)
    grads_both = swap(grads_far, "col")
    grads_near = swap(grads_here, "col")
    token, acts_here = tie(token, acts_here)
    send_g, keep_g = rotate([grads_here, grads_far, grads_near, grads_both], basis_out, 1, note(source_ids))
    got_g = swap(send_g, "seq", 1)
    acts_here, keep_g = tie(acts_here, keep_g)
    acts_far = swap(acts_here, "row")
    token, keep_g = stand(token, keep_g)
    token, acts_far, acts_here = tie(token, acts_far, acts_here)
    acts_both = swap(acts_far, "col")
    acts_near = swap(acts_here, "col")
    to_pair, to_both, to_x, keep_a = rotate([acts_here, acts_far, acts_near, acts_both], tiles, 3, flips=(1, 2))
    token, keep_a = tie(token, keep_a)
    token, got_g = tie(token, got_g)
    count = seqs * tok
    pair_g = small_call(pair_kernel, count + 16, keep_g, got_g, note(source_ids))
    token, pair_g, to_x = tie(token, pair_g, to_x)
    across_g = swap(pair_g, "seq", 2)
    from_both = lax.ppermute(
        to_both,
        ("seq", "row"),
        [(i * rows + j, (i ^ 1) * rows + (j ^ 1)) for i in range(seqs) for j in range(rows)],
    )
    from_pair = swap(to_pair, "seq", 1)
    from_x = swap(to_x, "row")
    (token,) = stand(token)
    token, from_x, from_pair, from_both = tie(token, from_x, from_pair, from_both)
    same, swapped = added(keep_a, from_pair), added(from_x, from_both)
    stay = jnp.where(x == high, same, swapped)
    cross = swap(jnp.where(x == high, swapped, same).astype(jnp.bfloat16), "seq", 2)
    token, across_g = tie(token, across_g)
    near_g = small_call(sum_kernel, count, pair_g, across_g)
    token, near_g = tie(token, near_g)
    far_g = swap(near_g, "seq", 1)
    (token,) = stand(token)
    token, cross = tie(token, cross)
    own_a = (stay + cross.astype(jnp.float32)).astype(jnp.bfloat16)
    quarters = plane_gather(own_a)

    ids = jnp.stack([source_ids, got_g[count, :tok], across_g[count, :tok], across_g[count + 1, :tok]])
    slot_ids = jnp.stack([lax.dynamic_index_in_dim(ids, u ^ s ^ j, keepdims=False) for j in range(seqs)])
    place = jnp.stack([u, low, 1 - low]).astype(jnp.int32)
    precond, value, flat, across, later = outer_near(place, quarters, near_g, eigvals)
    precond, slots = outer_far(place, flat, across, far_g, later, precond, value, token)
    chosen = slot_ids[None] == jnp.arange(SOURCES, dtype=jnp.bfloat16)[:, None, None]
    part = jnp.sum(jnp.where(chosen, slots[None], 0.0), axis=(1, 2))
    blocks = jnp.stack([lax.dynamic_index_in_dim(slots, u ^ j, keepdims=False) for j in range(seqs)])
    message = jnp.concatenate([blocks, jnp.broadcast_to(part[None, :], (seqs, SOURCES))], axis=1)
    message = jnp.broadcast_to(message[:, None, :], (seqs, rows * cols, tok + SOURCES))
    message = message.reshape(seqs * rows * cols, tok + SOURCES)
    parts = lax.all_to_all(message, PLANE, split_axis=0, concat_axis=0, tiled=True)
    scale_score = float(total_tokens) / float(width * width)
    vmem = pl.BlockSpec(memory_space=pltpu.VMEM)
    scores, influence = pl.pallas_call(
        functools.partial(finish_kernel, scale_score, scale_score * (float(SOURCES) / float(total_tokens))),
        out_shape=(jax.ShapeDtypeStruct((tok,), jnp.float32), jax.ShapeDtypeStruct((SOURCES,), jnp.float32)),
        in_specs=[vmem],
        out_specs=(vmem, vmem),
        compiler_params=pltpu.CompilerParams(vmem_limit_bytes=2**20),
        name="finish",
    )(parts)
    return (precond, scores, influence)


def solution(mesh):
    in_specs = (
        P(("grp", "seq"), ("row", "col")),
        P(("grp", "seq"), ("row", "col")),
        P(("grp", "seq")),
        P("seq", ("row", "col")),
        P("seq", ("row", "col")),
        P("seq", ("row", "col")),
    )
    out_specs = (P(("grp", "seq"), ("row", "col")), P(("grp", "seq")), P("grp"))
    fits = (mesh.shape["seq"], mesh.shape["row"], mesh.shape["col"]) == (4, 2, 2)
    local = local_pairs if fits else local_any
    return jax.shard_map(local, mesh=mesh, in_specs=in_specs, out_specs=out_specs, check_vma=False)
```
